512 devices in a mesh: step: 64 (over x, z), tp: 8 (over y, core).
Axes of the slice: x: 4, y: 4, z: 16, core: 2. Of those that a mesh axis runs over, the one named last changes fastest.
Arguments:
- latents: float32 [64, 256, 3072], P('step', None, 'tp'), may hold values from -6 to 6
- timesteps: int32 [65], replicated, may hold values from 0 to 3072, as said below
- start_offset: int32 [1], replicated, may hold values from 1 to 63
- slide_count: int32 [1], replicated, may hold values from 1 to 32
- mod_weight: bfloat16 [3, 256, 3072], P(None, None, 'tp'), may hold values from -2 to 2
- qkv_weight: bfloat16 [3, 3072, 2048], P(None, 'step', 'tp'), may hold values from -0.109375 to 0.109375
- out_weight: bfloat16 [2048, 3072], P('step', 'tp'), may hold values from -0.375 to 0.375
- q_gain: float32 [128], replicated
- k_gain: float32 [128], replicated
Outputs:
- updated: float32 [64, 256, 3072], P('step', None, 'tp')
The draws below stay inside these ranges and needn't reach their ends.
Inputs may be any that keep to these rules, and one draw needn't show every extreme that they name: Strictly falling from slot to slot; timesteps[0] = 3072 and timesteps[64] = 0.
All inputs are finite; a program needn't handle non-finite values.
Results may differ from the reference program's by a relative error of at most 0.008.
The reference program's roundings to bfloat16 on the way count: a program that leaves them out, or rounds other values in their place, can miss the bound.
Values may be sent and summed in bfloat16 or wider, within the bound.
No kernel may reach another device: no remote copies, remote signals or barrier semaphores. Data moves between devices by JAX's collectives and lax.ppermute only.
A program may use at most 128 MiB of HBM per device.

```python
import math
import jax
import jax.numpy as jnp
from jax import lax

D = 3072
HD = 128
FREQ = 256
HEADS = 16
TOK = 256
INNER = 2048
STEPS = 64
TGRID = 3072


def draw_timesteps(key, part):
    key = jax.random.fold_in(key, 11)
    gaps = jax.random.randint(key, (STEPS - 1,), 16, 49)
    falls = jnp.concatenate([jnp.zeros((1,), jnp.int32), jnp.cumsum(gaps).astype(jnp.int32)])
    upper = (48 * STEPS - falls).astype(jnp.int32)
    return jnp.concatenate([upper, jnp.zeros((1,), jnp.int32)]).astype(jnp.int32)


def gain_values(key, lowest, highest):
    unit = jax.random.uniform(key, (HD,), jnp.float32)
    return jnp.exp(jnp.log(lowest) + unit * (jnp.log(highest) - jnp.log(lowest))).astype(jnp.float32)


def draw_q_gain(key, part):
    key = jax.random.fold_in(key, 21)
    return gain_values(key, 0.6, 1.6)


def draw_k_gain(key, part):
    key = jax.random.fold_in(key, 31)
    return gain_values(key, 0.6, 1.6)


def block_scale(rng, extent, pieces, low, largest):
    def one(dim, shards_of):
        steps = jax.random.uniform(jax.random.fold_in(jax.random.fold_in(rng, 6), dim), (shards_of,), jnp.float32, low / len(pieces), largest / len(pieces))
        return jnp.repeat(jnp.exp(steps), extent[dim] // shards_of).reshape((-1,) + (1,) * (len(extent) - dim - 1))

    level = one(*pieces[0])
    for cut in pieces[1:]:
        level = level * one(*cut)
    return level


def centred(rng, dims, scale, limit, shards=(), kind=jnp.bfloat16):
    array = scale * jax.random.normal(rng, dims, jnp.float32)
    if shards:
        array = array * block_scale(rng, dims, shards, -0.22, 0.18)
    return jnp.clip(array, -limit, limit).astype(kind)


def setup_inputs(seed: int = 0) -> dict:
    streams_of = jax.random.split(jax.random.key(seed), 10)
    return {
        "latents": centred(streams_of[0], (STEPS, TOK, D), 1.0, 6.0, ((0, 64), (2, 8)), jnp.float32),
        "timesteps": draw_timesteps(jax.random.fold_in(streams_of[9], 71), 0),
        "start_offset": jax.random.randint(streams_of[2], (1,), 1, STEPS).astype(jnp.int32),
        "slide_count": jax.random.randint(streams_of[3], (1,), 1, STEPS // 2 + 1).astype(jnp.int32),
        "mod_weight": centred(streams_of[4], (3, FREQ, D), (2.0 * FREQ ** -0.5), 2.0, ((2, 8),)),
        "qkv_weight": centred(streams_of[5], (3, D, INNER), D ** -0.5, 0.109375, ((1, 64), (2, 8))),
        "out_weight": centred(streams_of[6], (INNER, D), (INNER // 8) ** -0.5, 0.375, ((0, 64), (1, 8))),
        "q_gain": draw_q_gain(jax.random.fold_in(streams_of[9], 71), 0),
        "k_gain": draw_k_gain(jax.random.fold_in(streams_of[9], 71), 0),
    }


def embed_time(tval):
    half = FREQ // 2
    freqs = jnp.exp(-math.log(10000.0) * jnp.arange(half, dtype=jnp.float32) / half)
    angles = 1000.0 * tval * freqs
    return jax.nn.silu(jnp.concatenate([jnp.cos(angles), jnp.sin(angles)])).astype(jnp.bfloat16)

def head_norm(values, gain):
    return values * lax.rsqrt(lax.optimization_barrier(jnp.mean(values * values, axis=-1, keepdims=True)) + 1e-06) * gain

def drift_of(latent, t_now, t_next, mod_weight, qkv_weight, out_weight, q_gain, k_gain):
    grid = jnp.float32(TGRID)
    tval = t_now.astype(jnp.float32) / grid
    step_dt = (t_now - t_next).astype(jnp.float32) / grid
    emb = embed_time(tval)
    mods = jnp.einsum('f,cfd->cd', emb.astype(jnp.float32), mod_weight.astype(jnp.float32)).astype(jnp.bfloat16)
    xf = latent.astype(jnp.bfloat16).astype(jnp.float32)
    mean = lax.optimization_barrier(jnp.mean(xf, axis=-1, keepdims=True))
    cent = xf - mean
    var = lax.optimization_barrier(jnp.mean(cent * cent, axis=-1, keepdims=True))
    normed = cent * lax.rsqrt(var + 1e-06)
    hidden = (normed * (1.0 + mods[1].astype(jnp.float32)) + mods[0].astype(jnp.float32)).astype(jnp.bfloat16)
    query = jnp.dot(hidden, qkv_weight[0], preferred_element_type=jnp.float32).reshape(TOK, HEADS, HD)
    keys = jnp.dot(hidden, qkv_weight[1], preferred_element_type=jnp.float32).reshape(TOK, HEADS, HD)
    vals = jnp.dot(hidden, qkv_weight[2], preferred_element_type=jnp.float32).reshape(TOK, HEADS, HD)
    qn = head_norm(query, q_gain).astype(jnp.bfloat16)
    kn = head_norm(keys, k_gain).astype(jnp.bfloat16)
    vb = vals.astype(jnp.bfloat16)
    scores = jnp.einsum('qhd,khd->hqk', qn.astype(jnp.float32), kn.astype(jnp.float32)) * HD ** (-0.5)
    scores = scores - lax.optimization_barrier(jnp.max(scores, axis=-1, keepdims=True))
    weights = jnp.exp(scores)
    probs = (weights / lax.optimization_barrier(jnp.sum(weights, axis=-1, keepdims=True))).astype(jnp.bfloat16)
    attn = jnp.einsum('hqk,khd->qhd', probs.astype(jnp.float32), vb.astype(jnp.float32))
    attn = attn.reshape(TOK, INNER).astype(jnp.bfloat16)
    proj = jnp.dot(attn, out_weight, preferred_element_type=jnp.float32)
    return step_dt * (mods[2].astype(jnp.float32) * proj)

def reference(latents, timesteps, start_offset, slide_count, mod_weight, qkv_weight, out_weight, q_gain, k_gain):
    start = start_offset[0]
    slide = slide_count[0]
    slots = jnp.arange(STEPS, dtype=jnp.int32)
    position = jnp.mod(slots - start + STEPS, STEPS).astype(jnp.int32)

    def one_slot(items):
        latent, t_now, t_next, where_pos = items
        drift = drift_of(latent, t_now, t_next, mod_weight, qkv_weight, out_weight, q_gain, k_gain)
        return drift + jnp.where(where_pos == 0, latent, jnp.zeros_like(latent))
    terms = lax.map(one_slot, (latents, timesteps[:-1], timesteps[1:], position))
    order = jnp.mod(slots + start, STEPS).astype(jnp.int32)
    ordered = jnp.take(terms, order, axis=0)
    running = jnp.cumsum(ordered, axis=0)
    before_pos = jnp.concatenate([jnp.zeros((1, TOK, D), jnp.float32), running[:-1]], axis=0)
    total = running[-1]
    before = jnp.take(before_pos, position, axis=0)
    moved = (position < slide)[:, None, None]
    return jnp.where(moved, total[None], before)
```

```python
import math

import jax
import jax.numpy as jnp
from jax import lax
from jax.experimental import pallas as pl
from jax.experimental.pallas import tpu as pltpu
from jax.sharding import Mesh
from jax.sharding import PartitionSpec as P

HD = 128
NX, NZ, NY, NC = 4, 16, 4, 2
STEP = ("x", "z")
TP = ("y", "c")
VMEM_LIMIT = 40 * 1024 * 1024


def shift(value, axis, size, by):
    return lax.ppermute(value, axis, [(i, (i + by) % size) for i in range(size)])


def swap_pair(value):
    return lax.ppermute(value, "x", [(i, i ^ 1) for i in range(NX)])


def swap_core(value):
    return lax.ppermute(value, "c", [(i, i ^ 1) for i in range(NC)])


def to_all(value, axis, size):
    return lax.all_to_all(jnp.broadcast_to(value[None], (size,) + value.shape), axis, 0, 0)


def embed_time(tvals, width):
    half = width // 2
    freqs = jnp.exp(-math.log(10000.0) * jnp.arange(half, dtype=jnp.float32) / half)
    angles = 1000.0 * tvals[:, None] * freqs
    both = jnp.concatenate([jnp.cos(angles), jnp.sin(angles)], axis=1)
    return jax.nn.silu(both).astype(jnp.bfloat16)


def pack_kernel(idx_ref, emb_ref, mod_ref, lat_ref, out_ref, gate_ref, mods_ref):
    tokens = lat_ref.shape[0]
    out_ref[0:tokens, :] = lat_ref[...].astype(jnp.bfloat16)
    emb = emb_ref[...]
    for i in range(3):
        mods = jnp.dot(emb, mod_ref[i], preferred_element_type=jnp.float32)
        mods = mods.astype(jnp.bfloat16).astype(jnp.float32)
        if i < 2:
            mods_ref[i] = mods
        else:
            gate_ref[...] = mods
    slot = idx_ref[5]
    tail = out_ref.shape[0] - tokens
    which = lax.broadcasted_iota(jnp.int32, (tail, lat_ref.shape[1]), 0)
    block = jnp.where(which == 0, mods_ref[0, pl.ds(slot, 1), :], 0.0)
    block = jnp.where(which == 1, mods_ref[1, pl.ds(slot, 1), :], block)
    out_ref[tokens:, :] = block.astype(jnp.bfloat16)


def sort_kernel(qkv_ref, out_ref, to_ref, sems):
    loads = []
    for dest in range(NX):
        at = pl.ds(dest % 2 * HD, HD)
        pairs = [(out_ref, to_ref.at[dest, 48:80])]
        for i in range(3):
            pairs.append((qkv_ref.at[i, :, at], to_ref.at[dest, 0:48, i * HD : (i + 1) * HD]))
        for i, (source, target) in enumerate(pairs):
            loads.append(pltpu.make_async_copy(source, target, sems.at[dest, i]))
    for load in loads:
        load.start()
    for load in loads:
        load.wait()


def norm_kernel(idx_ref, *refs):
    xs, h_ref = refs[:8], refs[8]
    y, c = idx_ref[2], idx_ref[3]
    tokens, width = h_ref.shape[1], xs[0].shape[2]
    features = 8 * width
    for slot in range(2):
        total = jnp.zeros((tokens, 1), jnp.float32)
        for part in xs:
            total += jnp.sum(part[slot, 0:tokens, :].astype(jnp.float32), axis=-1, keepdims=True)
        mean = total / features
        total = jnp.zeros((tokens, 1), jnp.float32)
        for part in xs:
            cent = part[slot, 0:tokens, :].astype(jnp.float32) - mean
            total += jnp.sum(cent * cent, axis=-1, keepdims=True)
        inv = lax.rsqrt(total / features + 1e-06)
        for j in range(NY):
            for i in range(NC):
                part = xs[NC * j + i]
                place = lax.rem(y + NY - j, NY) * NC + lax.rem(c + i, NC)
                mods = part[slot, tokens : tokens + 16, :].astype(jnp.float32)
                cent = part[slot, 0:tokens, :].astype(jnp.float32) - mean
                hidden = cent * inv * (1.0 + mods[1:2]) + mods[0:1]
                at = pl.ds(pl.multiple_of(place * width, 128), width)
                h_ref[slot, :, at] = hidden.astype(jnp.bfloat16)


def attention_kernel(idx_ref, qg_ref, kg_ref, h_ref, all_ref, o_ref, w_ref):
    odd = lax.rem(idx_ref[0], 2)
    for x in range(NX):
        for z in range(NZ):
            row = (x * NZ + z) * 48
            w_ref[row : row + 48, :] = all_ref[z, x, 0:48, :]
    for slot in range(2):
        qkv = jnp.dot(h_ref[slot], w_ref[...], preferred_element_type=jnp.float32)
        q = qkv[:, 0:HD]
        k = qkv[:, HD : 2 * HD]
        v = qkv[:, 2 * HD : 3 * HD].astype(jnp.bfloat16)
        qn = q * lax.rsqrt(jnp.mean(q * q, axis=-1, keepdims=True) + 1e-06) * qg_ref[...]
        kn = k * lax.rsqrt(jnp.mean(k * k, axis=-1, keepdims=True) + 1e-06) * kg_ref[...]
        scores = lax.dot_general(
            qn.astype(jnp.bfloat16),
            kn.astype(jnp.bfloat16),
            (((1,), (1,)), ((), ())),
            preferred_element_type=jnp.float32,
        ) * HD ** (-0.5)
        weights = jnp.exp(scores - jnp.max(scores, axis=-1, keepdims=True))
        probs = (weights / jnp.sum(weights, axis=-1, keepdims=True)).astype(jnp.bfloat16)
        out = jnp.dot(probs, v, preferred_element_type=jnp.float32)
        o_ref[lax.rem(odd + slot, 2)] = out.astype(jnp.bfloat16)


def project_kernel(idx_ref, win_ref, dt_ref, gate_ref, lat_ref, mine_ref, other_ref, all_ref, *refs):
    out_ref, a_ref, w_ref, term_ref, run_ref = refs
    c = idx_ref[3]
    start, slide = win_ref[0], win_ref[1]
    for j in range(NY):
        for i, part in enumerate((mine_ref, other_ref)):
            for n in range(2):
                head = (j * NC + lax.rem(c + i, NC)) * 2 + n
                at = pl.ds(pl.multiple_of(head * HD, HD), HD)
                for m in range(2):
                    row = (2 * m + n) * 128
                    a_ref[m * 128 : (m + 1) * 128, at] = part[j, row : row + 128, :]
    for x in range(NX):
        for z in range(NZ):
            row = (x * NZ + z) * 32
            w_ref[row : row + 32, :] = all_ref[z, x, 48:80, :]
    proj = jnp.dot(a_ref[...], w_ref[...], preferred_element_type=jnp.float32)
    for slot in range(NX * NZ):
        row = slot // (2 * NZ) * 128 + slot % NZ * 8 + slot // NZ % 2 * 4
        gate = gate_ref[slot : slot + 1, :]
        term_ref[slot] = dt_ref[slot] * (gate * proj[row : row + 4, :])
    term_ref[start] = term_ref[start] + lat_ref[lax.rem(start, NZ)]
    count = NX * NZ

    def step(i, run):
        slot = lax.rem(start + i, count)
        run_ref[slot] = run
        return run + term_ref[slot]

    total = lax.fori_loop(0, count, step, jnp.zeros(run_ref.shape[1:], jnp.float32))

    def move(i, _):
        run_ref[lax.rem(start + i, count)] = total
        return 0

    lax.fori_loop(0, slide, move, 0)
    runs = run_ref[...]
    largest = jnp.max(jnp.max(jnp.abs(runs), axis=0), keepdims=True)
    power = jnp.clip(jnp.ceil(jnp.log2(largest)), -100.0, 100.0) - 14.0
    width = runs.shape[2]
    out_ref[:, :, 0:width] = runs * jnp.exp2(-power)[None]
    rest = out_ref.shape[2] - width
    out_ref[:, :, width:] = jnp.broadcast_to(power[None], runs.shape[:2] + (rest,))


def unscale_kernel(in_ref, out_ref):
    count, rows = in_ref.shape[0], in_ref.shape[1]
    width = out_ref.shape[1]
    scale = jnp.exp2(in_ref[:, :, width : width + 128])
    for g in range(width // 128):
        values = in_ref[:, :, g * 128 : (g + 1) * 128] * scale
        for i in range(count):
            out_ref[i * rows : (i + 1) * rows, g * 128 : (g + 1) * 128] = values[i]


def vmem():
    return pl.BlockSpec(memory_space=pltpu.VMEM)


def smem():
    return pl.BlockSpec(memory_space=pltpu.SMEM)


def params():
    return pltpu.CompilerParams(vmem_limit_bytes=VMEM_LIMIT)


def per_device(
    latents,
    timesteps,
    start_offset,
    slide_count,
    mod_weight,
    qkv_weight,
    out_weight,
    q_gain,
    k_gain,
):
    x, z, y, c = (lax.axis_index(a) for a in ("x", "z", "y", "c"))
    slot = x * NZ + z
    count = NX * NZ
    start, slide = start_offset[0], slide_count[0]
    grid = jnp.float32(48 * count)
    times = timesteps.astype(jnp.float32)
    tvals = times[:-1] / grid
    step_dts = (timesteps[:-1] - timesteps[1:]).astype(jnp.float32) / grid
    local = latents[0]
    tokens, width = local.shape

    sorted_rows = pl.pallas_call(
        sort_kernel,
        out_shape=jax.ShapeDtypeStruct((NX, 80, 3 * HD), jnp.bfloat16),
        in_specs=[pl.BlockSpec(memory_space=pl.ANY)] * 2,
        out_specs=vmem(),
        scratch_shapes=[pltpu.SemaphoreType.DMA((NX, 4))],
        compiler_params=pltpu.CompilerParams(vmem_limit_bytes=61 * 1024 * 1024),
        name="sort",
    )(qkv_weight, out_weight)
    weights = lax.all_gather(lax.all_to_all(sorted_rows, "x", 0, 0, tiled=True), "z")

    idx = jnp.stack([x, z, y, c, start, slot]).astype(jnp.int32)
    emb = embed_time(tvals, mod_weight.shape[1])
    packed, gates = pl.pallas_call(
        pack_kernel,
        out_shape=(
            jax.ShapeDtypeStruct((tokens + 16, width), jnp.bfloat16),
            jax.ShapeDtypeStruct((count, width), jnp.float32),
        ),
        in_specs=[smem()] + [vmem()] * 3,
        out_specs=(vmem(), vmem()),
        scratch_shapes=[pltpu.VMEM((2, count, width), jnp.float32)],
        compiler_params=params(),
        name="pack",
    )(idx, emb, mod_weight, local)
    both = jnp.stack([packed, swap_pair(packed)])
    xs = [both] + [shift(both, "y", NY, j) for j in range(1, NY)]
    xs = [b for mine in xs for b in (mine, swap_core(mine))]
    hidden = pl.pallas_call(
        norm_kernel,
        out_shape=jax.ShapeDtypeStruct((2, tokens, 8 * width), jnp.bfloat16),
        in_specs=[smem()] + [vmem()] * 8,
        out_specs=vmem(),
        compiler_params=params(),
        name="norm",
    )(idx, *xs)

    rows = tokens // count
    first = lax.all_to_all(local.reshape(NX, tokens // NX, width), "x", 0, 0, tiled=True)
    first = lax.dynamic_index_in_dim(first, start // NZ, 0, keepdims=False)
    first = lax.all_to_all(first.reshape(NZ, rows, width), "z", 0, 0, tiled=True)
    first, hidden = lax.optimization_barrier((first, hidden))
    attn = pl.pallas_call(
        attention_kernel,
        out_shape=jax.ShapeDtypeStruct((2, tokens, HD), jnp.bfloat16),
        in_specs=[smem()] + [vmem()] * 4,
        out_specs=vmem(),
        scratch_shapes=[pltpu.VMEM((48 * count, 3 * HD), jnp.bfloat16)],
        compiler_params=params(),
        name="attention",
    )(idx, q_gain[None], k_gain[None], hidden, weights)
    attn = attn.reshape(2, count, rows, HD).transpose(1, 0, 2, 3).reshape(count, 2 * rows, HD)
    attn = lax.all_to_all(attn, STEP, 0, 0, tiled=True).reshape(count * 2 * rows, HD)
    mine = to_all(attn, "y", NY)
    sums = pl.pallas_call(
        project_kernel,
        out_shape=jax.ShapeDtypeStruct((count, rows, width + 128), jnp.float32),
        in_specs=[smem()] * 3 + [vmem()] * 5,
        out_specs=vmem(),
        scratch_shapes=[
            pltpu.VMEM((tokens, 2048), jnp.bfloat16),
            pltpu.VMEM((2048, width), jnp.bfloat16),
            pltpu.VMEM((count, rows, width), jnp.float32),
            pltpu.VMEM((count, rows, width), jnp.float32),
        ],
        compiler_params=params(),
        name="project",
    )(idx, jnp.stack([start, slide]), step_dts, gates, first, mine, swap_core(mine), weights)
    back = lax.all_to_all(sums.astype(jnp.float16), STEP, 0, 0, tiled=True).astype(jnp.float32)
    return pl.pallas_call(
        unscale_kernel,
        out_shape=jax.ShapeDtypeStruct((tokens, width), jnp.float32),
        in_specs=[vmem()],
        out_specs=vmem(),
        compiler_params=params(),
        name="unscale",
    )(back)[None]


def solution(mesh):
    fine = Mesh(mesh.devices.reshape(NX, NZ, NY, NC), ("x", "z", "y", "c"))
    return jax.shard_map(
        per_device,
        mesh=fine,
        in_specs=(
            P(STEP, None, TP),
            P(),
            P(),
            P(),
            P(None, None, TP),
            P(None, STEP, TP),
            P(STEP, TP),
            P(),
            P(),
        ),
        out_specs=P(STEP, None, TP),
        check_vma=False,
    )
```

```python
import math

import jax
import jax.numpy as jnp
from jax import lax
from jax.experimental import pallas as pl
from jax.experimental.pallas import tpu as pltpu
from jax.sharding import Mesh
from jax.sharding import PartitionSpec as P

HD = 128
NX, NZ, NY, NC = 4, 16, 4, 2
STEP = ("x", "z")
TP = ("y", "c")
VMEM_LIMIT = 40 * 1024 * 1024


def shift(value, axis, size, by):
    return lax.ppermute(value, axis, [(i, (i + by) % size) for i in range(size)])


def swap_pair(value):
    return lax.ppermute(value, "x", [(i, i ^ 1) for i in range(NX)])


def swap_core(value):
    return lax.ppermute(value, "c", [(i, i ^ 1) for i in range(NC)])


def to_all(value, axis, size):
    return lax.all_to_all(jnp.broadcast_to(value[None], (size,) + value.shape), axis, 0, 0)


def embed_time(tvals, width):
    half = width // 2
    freqs = jnp.exp(-math.log(10000.0) * jnp.arange(half, dtype=jnp.float32) / half)
    angles = 1000.0 * tvals[:, None] * freqs
    both = jnp.concatenate([jnp.cos(angles), jnp.sin(angles)], axis=1)
    return jax.nn.silu(both).astype(jnp.bfloat16)


def pack_kernel(idx_ref, emb_ref, mod_ref, lat_ref, out_ref, gate_ref, mods_ref):
    tokens = lat_ref.shape[0]
    out_ref[0:tokens, :] = lat_ref[...].astype(jnp.bfloat16)
    emb = emb_ref[...]
    for i in range(3):
        mods = jnp.dot(emb, mod_ref[i], preferred_element_type=jnp.float32)
        mods = mods.astype(jnp.bfloat16).astype(jnp.float32)
        if i < 2:
            mods_ref[i] = mods
        else:
            gate_ref[...] = mods
    slot = idx_ref[5]
    tail = out_ref.shape[0] - tokens
    which = lax.broadcasted_iota(jnp.int32, (tail, lat_ref.shape[1]), 0)
    block = jnp.where(which == 0, mods_ref[0, pl.ds(slot, 1), :], 0.0)
    block = jnp.where(which == 1, mods_ref[1, pl.ds(slot, 1), :], block)
    out_ref[tokens:, :] = block.astype(jnp.bfloat16)


def sort_kernel(qkv_hbm, out_hbm, to_ref, qkv_ref, out_ref, sems):
    loads = [
        pltpu.make_async_copy(qkv_hbm, qkv_ref, sems.at[0]),
        pltpu.make_async_copy(out_hbm, out_ref, sems.at[1]),
    ]
    for load in loads:
        load.start()
    for load in loads:
        load.wait()
    for dest in range(NX):
        head = dest % 2
        for i in range(3):
            to_ref[dest, 0:48, i * HD : (i + 1) * HD] = qkv_ref[i, :, head * HD : (head + 1) * HD]
        to_ref[dest, 48:80, :] = out_ref[...]


def order_kernel(all_ref, to_ref):
    for x in range(NX):
        for z in range(NZ):
            row = (x * NZ + z) * 32
            to_ref[row : row + 32, :] = all_ref[z, x, 48:80, :]


def norm_kernel(idx_ref, mine_ref, other_ref, h_ref):
    c = idx_ref[3]
    xs = [ref.at[j] for j in range(NY) for ref in (mine_ref, other_ref)]
    tokens, width = h_ref.shape[1], mine_ref.shape[3]
    features = 8 * width
    for slot in range(2):
        total = jnp.zeros((tokens, 1), jnp.float32)
        for part in xs:
            total += jnp.sum(part[slot, 0:tokens, :].astype(jnp.float32), axis=-1, keepdims=True)
        mean = total / features
        total = jnp.zeros((tokens, 1), jnp.float32)
        for part in xs:
            cent = part[slot, 0:tokens, :].astype(jnp.float32) - mean
            total += jnp.sum(cent * cent, axis=-1, keepdims=True)
        inv = lax.rsqrt(total / features + 1e-06)
        for j in range(NY):
            for i in range(NC):
                part = xs[NC * j + i]
                place = j * NC + lax.rem(c + i, NC)
                mods = part[slot, tokens : tokens + 16, :].astype(jnp.float32)
                cent = part[slot, 0:tokens, :].astype(jnp.float32) - mean
                hidden = cent * inv * (1.0 + mods[1:2]) + mods[0:1]
                at = pl.ds(pl.multiple_of(place * width, 128), width)
                h_ref[slot, :, at] = hidden.astype(jnp.bfloat16)


def attention_kernel(idx_ref, qg_ref, kg_ref, h_ref, all_ref, o_ref, w_ref):
    odd = lax.rem(idx_ref[0], 2)
    for x in range(NX):
        for z in range(NZ):
            row = (x * NZ + z) * 48
            w_ref[row : row + 48, :] = all_ref[z, x, 0:48, :]
    for slot in range(2):
        qkv = jnp.dot(h_ref[slot], w_ref[...], preferred_element_type=jnp.float32)
        q = qkv[:, 0:HD]
        k = qkv[:, HD : 2 * HD]
        v = qkv[:, 2 * HD : 3 * HD].astype(jnp.bfloat16)
        qn = q * lax.rsqrt(jnp.mean(q * q, axis=-1, keepdims=True) + 1e-06) * qg_ref[...]
        kn = k * lax.rsqrt(jnp.mean(k * k, axis=-1, keepdims=True) + 1e-06) * kg_ref[...]
        scores = lax.dot_general(
            qn.astype(jnp.bfloat16),
            kn.astype(jnp.bfloat16),
            (((1,), (1,)), ((), ())),
            preferred_element_type=jnp.float32,
        ) * HD ** (-0.5)
        weights = jnp.exp(scores - jnp.max(scores, axis=-1, keepdims=True))
        probs = (weights / jnp.sum(weights, axis=-1, keepdims=True)).astype(jnp.bfloat16)
        out = jnp.dot(probs, v, preferred_element_type=jnp.float32)
        o_ref[lax.rem(odd + slot, 2)] = out.astype(jnp.bfloat16)


def project_kernel(idx_ref, win_ref, dt_ref, gate_ref, lat_ref, mine_ref, other_ref, w_ref, *refs):
    out_ref, a_ref, term_ref, run_ref = refs
    c = idx_ref[3]
    start, slide = win_ref[0], win_ref[1]
    for j in range(NY):
        for i, part in enumerate((mine_ref, other_ref)):
            for n in range(2):
                head = (j * NC + lax.rem(c + i, NC)) * 2 + n
                at = pl.ds(pl.multiple_of(head * HD, HD), HD)
                for m in range(2):
                    row = (2 * m + n) * 128
                    a_ref[m * 128 : (m + 1) * 128, at] = part[j, row : row + 128, :]
    proj = jnp.dot(a_ref[...], w_ref[...], preferred_element_type=jnp.float32)
    for slot in range(NX * NZ):
        row = slot // (2 * NZ) * 128 + slot % NZ * 8 + slot // NZ % 2 * 4
        gate = gate_ref[slot : slot + 1, :]
        term_ref[slot] = dt_ref[slot] * (gate * proj[row : row + 4, :])
    term_ref[start] = term_ref[start] + lat_ref[lax.rem(start, NZ)]
    count = NX * NZ

    def step(i, run):
        slot = lax.rem(start + i, count)
        run_ref[slot] = run
        return run + term_ref[slot]

    total = lax.fori_loop(
        0, count, step, jnp.zeros(run_ref.shape[1:], jnp.float32), unroll=8
    )

    def move(i, _):
        run_ref[lax.rem(start + i, count)] = total
        return 0

    lax.fori_loop(0, slide, move, 0)
    runs = run_ref[...]
    largest = jnp.max(jnp.max(jnp.abs(runs), axis=0), keepdims=True)
    power = jnp.clip(jnp.ceil(jnp.log2(largest)), -100.0, 100.0) - 14.0
    width = runs.shape[2]
    out_ref[:, :, 0:width] = runs * jnp.exp2(-power)[None]
    rest = out_ref.shape[2] - width
    out_ref[:, :, width:] = jnp.broadcast_to(power[None], runs.shape[:2] + (rest,))


def unscale_kernel(in_ref, out_ref):
    count, rows = in_ref.shape[0], in_ref.shape[1]
    width = out_ref.shape[1]
    scale = jnp.exp2(in_ref[:, :, width : width + 128])
    for g in range(width // 128):
        values = in_ref[:, :, g * 128 : (g + 1) * 128] * scale
        for i in range(count):
            out_ref[i * rows : (i + 1) * rows, g * 128 : (g + 1) * 128] = values[i]


def vmem():
    return pl.BlockSpec(memory_space=pltpu.VMEM)


def smem():
    return pl.BlockSpec(memory_space=pltpu.SMEM)


def params():
    return pltpu.CompilerParams(vmem_limit_bytes=VMEM_LIMIT)


def per_device(
    latents,
    timesteps,
    start_offset,
    slide_count,
    mod_weight,
    qkv_weight,
    out_weight,
    q_gain,
    k_gain,
):
    x, z, y, c = (lax.axis_index(a) for a in ("x", "z", "y", "c"))
    slot = x * NZ + z
    count = NX * NZ
    start, slide = start_offset[0], slide_count[0]
    grid = jnp.float32(48 * count)
    times = timesteps.astype(jnp.float32)
    tvals = times[:-1] / grid
    step_dts = (timesteps[:-1] - timesteps[1:]).astype(jnp.float32) / grid
    local = latents[0]
    tokens, width = local.shape

    sorted_rows = pl.pallas_call(
        sort_kernel,
        out_shape=jax.ShapeDtypeStruct((NX, 80, 3 * HD), jnp.bfloat16),
        in_specs=[pl.BlockSpec(memory_space=pl.ANY)] * 2,
        out_specs=vmem(),
        scratch_shapes=[
            pltpu.VMEM(qkv_weight.shape, jnp.bfloat16),
            pltpu.VMEM(out_weight.shape, jnp.bfloat16),
            pltpu.SemaphoreType.DMA((2,)),
        ],
        compiler_params=pltpu.CompilerParams(vmem_limit_bytes=61 * 1024 * 1024),
        name="sort",
    )(qkv_weight, out_weight)
    weights = lax.all_gather(lax.all_to_all(sorted_rows, "x", 0, 0, tiled=True), "z")

    idx = jnp.stack([x, z, y, c, start, slot]).astype(jnp.int32)
    emb = embed_time(tvals, mod_weight.shape[1])
    packed, gates = pl.pallas_call(
        pack_kernel,
        out_shape=(
            jax.ShapeDtypeStruct((tokens + 16, width), jnp.bfloat16),
            jax.ShapeDtypeStruct((count, width), jnp.float32),
        ),
        in_specs=[smem()] + [vmem()] * 3,
        out_specs=(vmem(), vmem()),
        scratch_shapes=[pltpu.VMEM((2, count, width), jnp.float32)],
        compiler_params=params(),
        name="pack",
    )(idx, emb, mod_weight, local)
    everywhere = to_all(jnp.stack([packed, swap_pair(packed)]), "y", NY)
    hidden = pl.pallas_call(
        norm_kernel,
        out_shape=jax.ShapeDtypeStruct((2, tokens, 8 * width), jnp.bfloat16),
        in_specs=[smem()] + [vmem()] * 2,
        out_specs=vmem(),
        compiler_params=params(),
        name="norm",
    )(idx, everywhere, swap_core(everywhere))

    rows = tokens // count
    first = local.astype(jnp.float16).reshape(NX, tokens // NX, width)
    first = lax.all_to_all(first, "x", 0, 0, tiled=True)
    first = lax.dynamic_index_in_dim(first, start // NZ, 0, keepdims=False)
    first = lax.all_to_all(first.reshape(NZ, rows, width), "z", 0, 0, tiled=True)
    first = first.astype(jnp.float32)
    first, hidden = lax.optimization_barrier((first, hidden))
    attn = pl.pallas_call(
        attention_kernel,
        out_shape=jax.ShapeDtypeStruct((2, tokens, HD), jnp.bfloat16),
        in_specs=[smem()] + [vmem()] * 4,
        out_specs=vmem(),
        scratch_shapes=[pltpu.VMEM((48 * count, 3 * HD), jnp.bfloat16)],
        compiler_params=params(),
        name="attention",
    )(idx, q_gain[None], k_gain[None], hidden, weights)
    attn = attn.reshape(2, count, rows, HD).transpose(1, 0, 2, 3).reshape(count, 2 * rows, HD)
    attn = lax.all_to_all(attn, STEP, 0, 0, tiled=True).reshape(count * 2 * rows, HD)
    mine = to_all(attn, "y", NY)
    out_rows = pl.pallas_call(
        order_kernel,
        out_shape=jax.ShapeDtypeStruct((2048, width), jnp.bfloat16),
        in_specs=[vmem()],
        out_specs=vmem(),
        compiler_params=params(),
        name="order",
    )(weights)
    sums = pl.pallas_call(
        project_kernel,
        out_shape=jax.ShapeDtypeStruct((count, rows, width + 128), jnp.float32),
        in_specs=[smem()] * 3 + [vmem()] * 5,
        out_specs=vmem(),
        scratch_shapes=[
            pltpu.VMEM((tokens, 2048), jnp.bfloat16),
            pltpu.VMEM((count, rows, width), jnp.float32),
            pltpu.VMEM((count, rows, width), jnp.float32),
        ],
        compiler_params=params(),
        name="project",
    )(idx, jnp.stack([start, slide]), step_dts, gates, first, mine, swap_core(mine), out_rows)
    back = lax.all_to_all(sums.astype(jnp.float16), STEP, 0, 0, tiled=True).astype(jnp.float32)
    return pl.pallas_call(
        unscale_kernel,
        out_shape=jax.ShapeDtypeStruct((tokens, width), jnp.float32),
        in_specs=[vmem()],
        out_specs=vmem(),
        compiler_params=params(),
        name="unscale",
    )(back)[None]


def solution(mesh):
    fine = Mesh(mesh.devices.reshape(NX, NZ, NY, NC), ("x", "z", "y", "c"))
    return jax.shard_map(
        per_device,
        mesh=fine,
        in_specs=(
            P(STEP, None, TP),
            P(),
            P(),
            P(),
            P(None, None, TP),
            P(None, STEP, TP),
            P(STEP, TP),
            P(),
            P(),
        ),
        out_specs=P(STEP, None, TP),
        check_vma=False,
    )
```

```python
import math

import jax
import jax.numpy as jnp
from jax import lax
from jax.experimental import pallas as pl
from jax.experimental.pallas import tpu as pltpu
from jax.sharding import Mesh
from jax.sharding import PartitionSpec as P

HD = 128
NX, NZ, NY, NC = 4, 16, 4, 2
STEP = ("x", "z")
TP = ("y", "c")
VMEM_LIMIT = 40 * 1024 * 1024


def shift(value, axis, size, by):
    return lax.ppermute(value, axis, [(i, (i + by) % size) for i in range(size)])


def swap_pair(value):
    return lax.ppermute(value, "x", [(i, i ^ 1) for i in range(NX)])


def swap_core(value):
    return lax.ppermute(value, "c", [(i, i ^ 1) for i in range(NC)])


def to_all(value, axis, size):
    return lax.all_to_all(jnp.broadcast_to(value[None], (size,) + value.shape), axis, 0, 0)


def embed_time(tvals, width):
    half = width // 2
    freqs = jnp.exp(-math.log(10000.0) * jnp.arange(half, dtype=jnp.float32) / half)
    angles = 1000.0 * tvals[:, None] * freqs
    both = jnp.concatenate([jnp.cos(angles), jnp.sin(angles)], axis=1)
    return jax.nn.silu(both).astype(jnp.bfloat16)


def pack_kernel(idx_ref, emb_ref, mod_ref, lat_ref, out_ref, gate_ref, mods_ref):
    tokens = lat_ref.shape[0]
    out_ref[0:tokens, :] = lat_ref[...].astype(jnp.bfloat16)
    emb = emb_ref[...]
    for i in range(3):
        mods = jnp.dot(emb, mod_ref[i], preferred_element_type=jnp.float32)
        mods = mods.astype(jnp.bfloat16).astype(jnp.float32)
        if i < 2:
            mods_ref[i] = mods
        else:
            gate_ref[...] = mods
    slot = idx_ref[5]
    tail = out_ref.shape[0] - tokens
    which = lax.broadcasted_iota(jnp.int32, (tail, lat_ref.shape[1]), 0)
    block = jnp.where(which == 0, mods_ref[0, pl.ds(slot, 1), :], 0.0)
    block = jnp.where(which == 1, mods_ref[1, pl.ds(slot, 1), :], block)
    out_ref[tokens:, :] = block.astype(jnp.bfloat16)


def sort_kernel(qkv_hbm, out_hbm, to_ref, qkv_ref, out_ref, sems):
    loads = [
        pltpu.make_async_copy(qkv_hbm, qkv_ref, sems.at[0]),
        pltpu.make_async_copy(out_hbm, out_ref, sems.at[1]),
    ]
    for load in loads:
        load.start()
    for load in loads:
        load.wait()
    for dest in range(NX):
        head = dest % 2
        for i in range(3):
            to_ref[dest, 0:48, i * HD : (i + 1) * HD] = qkv_ref[i, :, head * HD : (head + 1) * HD]
        to_ref[dest, 48:80, :] = out_ref[...]


def order_kernel(all_ref, to_ref):
    for x in range(NX):
        for z in range(NZ):
            row = (x * NZ + z) * 32
            to_ref[row : row + 32, :] = all_ref[z, x, 48:80, :]


def norm_kernel(idx_ref, *refs):
    xs, h_ref = refs[:8], refs[8]
    y, c = idx_ref[2], idx_ref[3]
    tokens, width = h_ref.shape[1], xs[0].shape[2]
    features = 8 * width
    for slot in range(2):
        total = jnp.zeros((tokens, 1), jnp.float32)
        for part in xs:
            total += jnp.sum(part[slot, 0:tokens, :].astype(jnp.float32), axis=-1, keepdims=True)
        mean = total / features
        total = jnp.zeros((tokens, 1), jnp.float32)
        for part in xs:
            cent = part[slot, 0:tokens, :].astype(jnp.float32) - mean
            total += jnp.sum(cent * cent, axis=-1, keepdims=True)
        inv = lax.rsqrt(total / features + 1e-06)
        for j in range(NY):
            for i in range(NC):
                part = xs[NC * j + i]
                place = lax.rem(y + NY - j, NY) * NC + lax.rem(c + i, NC)
                mods = part[slot, tokens : tokens + 16, :].astype(jnp.float32)
                cent = part[slot, 0:tokens, :].astype(jnp.float32) - mean
                hidden = cent * inv * (1.0 + mods[1:2]) + mods[0:1]
                at = pl.ds(pl.multiple_of(place * width, 128), width)
                h_ref[slot, :, at] = hidden.astype(jnp.bfloat16)


def attention_kernel(idx_ref, qg_ref, kg_ref, h_ref, all_ref, o_ref, w_ref):
    odd = lax.rem(idx_ref[0], 2)
    for x in range(NX):
        for z in range(NZ):
            row = (x * NZ + z) * 48
            w_ref[row : row + 48, :] = all_ref[z, x, 0:48, :]
    for slot in range(2):
        qkv = jnp.dot(h_ref[slot], w_ref[...], preferred_element_type=jnp.float32)
        q = qkv[:, 0:HD]
        k = qkv[:, HD : 2 * HD]
        v = qkv[:, 2 * HD : 3 * HD].astype(jnp.bfloat16)
        qn = q * lax.rsqrt(jnp.mean(q * q, axis=-1, keepdims=True) + 1e-06) * qg_ref[...]
        kn = k * lax.rsqrt(jnp.mean(k * k, axis=-1, keepdims=True) + 1e-06) * kg_ref[...]
        scores = lax.dot_general(
            qn.astype(jnp.bfloat16),
            kn.astype(jnp.bfloat16),
            (((1,), (1,)), ((), ())),
            preferred_element_type=jnp.float32,
        ) * HD ** (-0.5)
        weights = jnp.exp(scores - jnp.max(scores, axis=-1, keepdims=True))
        probs = (weights / jnp.sum(weights, axis=-1, keepdims=True)).astype(jnp.bfloat16)
        out = jnp.dot(probs, v, preferred_element_type=jnp.float32)
        o_ref[lax.rem(odd + slot, 2)] = out.astype(jnp.bfloat16)


def project_kernel(idx_ref, win_ref, dt_ref, gate_ref, lat_ref, mine_ref, other_ref, w_ref, *refs):
    out_ref, a_ref, term_ref, run_ref = refs
    c = idx_ref[3]
    start, slide = win_ref[0], win_ref[1]
    for j in range(NY):
        for i, part in enumerate((mine_ref, other_ref)):
            for n in range(2):
                head = (j * NC + lax.rem(c + i, NC)) * 2 + n
                at = pl.ds(pl.multiple_of(head * HD, HD), HD)
                for m in range(2):
                    row = (2 * m + n) * 128
                    a_ref[m * 128 : (m + 1) * 128, at] = part[j, row : row + 128, :]
    proj = jnp.dot(a_ref[...], w_ref[...], preferred_element_type=jnp.float32)
    for slot in range(NX * NZ):
        row = slot // (2 * NZ) * 128 + slot % NZ * 8 + slot // NZ % 2 * 4
        gate = gate_ref[slot : slot + 1, :]
        term_ref[slot] = dt_ref[slot] * (gate * proj[row : row + 4, :])
    term_ref[start] = term_ref[start] + lat_ref[lax.rem(start, NZ)]
    count = NX * NZ

    def step(i, run):
        slot = lax.rem(start + i, count)
        run_ref[slot] = run
        return run + term_ref[slot]

    total = lax.fori_loop(
        0, count, step, jnp.zeros(run_ref.shape[1:], jnp.float32), unroll=8
    )

    def move(i, _):
        run_ref[lax.rem(start + i, count)] = total
        return 0

    lax.fori_loop(0, slide, move, 0)
    runs = run_ref[...]
    largest = jnp.max(jnp.max(jnp.abs(runs), axis=0), keepdims=True)
    power = jnp.clip(jnp.ceil(jnp.log2(largest)), -100.0, 100.0) - 14.0
    width = runs.shape[2]
    out_ref[:, :, 0:width] = runs * jnp.exp2(-power)[None]
    rest = out_ref.shape[2] - width
    out_ref[:, :, width:] = jnp.broadcast_to(power[None], runs.shape[:2] + (rest,))


def unscale_kernel(in_ref, out_ref):
    count, rows = in_ref.shape[0], in_ref.shape[1]
    width = out_ref.shape[1]
    scale = jnp.exp2(in_ref[:, :, width : width + 128])
    for g in range(width // 128):
        values = in_ref[:, :, g * 128 : (g + 1) * 128] * scale
        for i in range(count):
            out_ref[i * rows : (i + 1) * rows, g * 128 : (g + 1) * 128] = values[i]


def vmem():
    return pl.BlockSpec(memory_space=pltpu.VMEM)


def smem():
    return pl.BlockSpec(memory_space=pltpu.SMEM)


def params():
    return pltpu.CompilerParams(vmem_limit_bytes=VMEM_LIMIT)


def per_device(
    latents,
    timesteps,
    start_offset,
    slide_count,
    mod_weight,
    qkv_weight,
    out_weight,
    q_gain,
    k_gain,
):
    x, z, y, c = (lax.axis_index(a) for a in ("x", "z", "y", "c"))
    slot = x * NZ + z
    count = NX * NZ
    start, slide = start_offset[0], slide_count[0]
    grid = jnp.float32(48 * count)
    times = timesteps.astype(jnp.float32)
    tvals = times[:-1] / grid
    step_dts = (timesteps[:-1] - timesteps[1:]).astype(jnp.float32) / grid
    local = latents[0]
    tokens, width = local.shape

    sorted_rows = pl.pallas_call(
        sort_kernel,
        out_shape=jax.ShapeDtypeStruct((NX, 80, 3 * HD), jnp.bfloat16),
        in_specs=[pl.BlockSpec(memory_space=pl.ANY)] * 2,
        out_specs=vmem(),
        scratch_shapes=[
            pltpu.VMEM(qkv_weight.shape, jnp.bfloat16),
            pltpu.VMEM(out_weight.shape, jnp.bfloat16),
            pltpu.SemaphoreType.DMA((2,)),
        ],
        compiler_params=pltpu.CompilerParams(vmem_limit_bytes=61 * 1024 * 1024),
        name="sort",
    )(qkv_weight, out_weight)
    weights = lax.all_gather(lax.all_to_all(sorted_rows, "x", 0, 0, tiled=True), "z")

    idx = jnp.stack([x, z, y, c, start, slot]).astype(jnp.int32)
    emb = embed_time(tvals, mod_weight.shape[1])
    packed, gates = pl.pallas_call(
        pack_kernel,
        out_shape=(
            jax.ShapeDtypeStruct((tokens + 16, width), jnp.bfloat16),
            jax.ShapeDtypeStruct((count, width), jnp.float32),
        ),
        in_specs=[smem()] + [vmem()] * 3,
        out_specs=(vmem(), vmem()),
        scratch_shapes=[pltpu.VMEM((2, count, width), jnp.float32)],
        compiler_params=params(),
        name="pack",
    )(idx, emb, mod_weight, local)
    both = jnp.stack([packed, swap_pair(packed)])
    xs = [both] + [shift(both, "y", NY, j) for j in range(1, NY)]
    xs = [b for mine in xs for b in (mine, swap_core(mine))]
    hidden = pl.pallas_call(
        norm_kernel,
        out_shape=jax.ShapeDtypeStruct((2, tokens, 8 * width), jnp.bfloat16),
        in_specs=[smem()] + [vmem()] * 8,
        out_specs=vmem(),
        compiler_params=params(),
        name="norm",
    )(idx, *xs)

    rows = tokens // count
    first = local.astype(jnp.float16).reshape(NX, tokens // NX, width)
    first = lax.all_to_all(first, "x", 0, 0, tiled=True)
    first = lax.dynamic_index_in_dim(first, start // NZ, 0, keepdims=False)
    first = lax.all_to_all(first.reshape(NZ, rows, width), "z", 0, 0, tiled=True)
    first = first.astype(jnp.float32)
    first, hidden = lax.optimization_barrier((first, hidden))
    attn = pl.pallas_call(
        attention_kernel,
        out_shape=jax.ShapeDtypeStruct((2, tokens, HD), jnp.bfloat16),
        in_specs=[smem()] + [vmem()] * 4,
        out_specs=vmem(),
        scratch_shapes=[pltpu.VMEM((48 * count, 3 * HD), jnp.bfloat16)],
        compiler_params=params(),
        name="attention",
    )(idx, q_gain[None], k_gain[None], hidden, weights)
    attn = attn.reshape(2, count, rows, HD).transpose(1, 0, 2, 3).reshape(count, 2 * rows, HD)
    attn = lax.all_to_all(attn, STEP, 0, 0, tiled=True).reshape(count * 2 * rows, HD)
    mine = to_all(attn, "y", NY)
    out_rows = pl.pallas_call(
        order_kernel,
        out_shape=jax.ShapeDtypeStruct((2048, width), jnp.bfloat16),
        in_specs=[vmem()],
        out_specs=vmem(),
        compiler_params=params(),
        name="order",
    )(weights)
    sums = pl.pallas_call(
        project_kernel,
        out_shape=jax.ShapeDtypeStruct((count, rows, width + 128), jnp.float32),
        in_specs=[smem()] * 3 + [vmem()] * 5,
        out_specs=vmem(),
        scratch_shapes=[
            pltpu.VMEM((tokens, 2048), jnp.bfloat16),
            pltpu.VMEM((count, rows, width), jnp.float32),
            pltpu.VMEM((count, rows, width), jnp.float32),
        ],
        compiler_params=params(),
        name="project",
    )(idx, jnp.stack([start, slide]), step_dts, gates, first, mine, swap_core(mine), out_rows)
    back = lax.all_to_all(sums.astype(jnp.float16), STEP, 0, 0, tiled=True).astype(jnp.float32)
    return pl.pallas_call(
        unscale_kernel,
        out_shape=jax.ShapeDtypeStruct((tokens, width), jnp.float32),
        in_specs=[vmem()],
        out_specs=vmem(),
        compiler_params=params(),
        name="unscale",
    )(back)[None]


def solution(mesh):
    fine = Mesh(mesh.devices.reshape(NX, NZ, NY, NC), ("x", "z", "y", "c"))
    return jax.shard_map(
        per_device,
        mesh=fine,
        in_specs=(
            P(STEP, None, TP),
            P(),
            P(),
            P(),
            P(None, None, TP),
            P(None, STEP, TP),
            P(STEP, TP),
            P(),
            P(),
        ),
        out_specs=P(STEP, None, TP),
        check_vma=False,
    )
```

```python
import math

import jax
import jax.numpy as jnp
from jax import lax
from jax.experimental import pallas as pl
from jax.experimental.pallas import tpu as pltpu
from jax.sharding import Mesh
from jax.sharding import PartitionSpec as P

HD = 128
NX, NZ, NY, NC = 4, 16, 4, 2
STEP = ("x", "z")
TP = ("y", "c")
VMEM_LIMIT = 40 * 1024 * 1024


def shift(value, axis, size, by):
    return lax.ppermute(value, axis, [(i, (i + by) % size) for i in range(size)])


def swap_pair(value):
    return lax.ppermute(value, "x", [(i, i ^ 1) for i in range(NX)])


def swap_core(value):
    return lax.ppermute(value, "c", [(i, i ^ 1) for i in range(NC)])


def to_all(value, axis, size):
    return lax.all_to_all(jnp.broadcast_to(value[None], (size,) + value.shape), axis, 0, 0)


def embed_time(tvals, width):
    half = width // 2
    freqs = jnp.exp(-math.log(10000.0) * jnp.arange(half, dtype=jnp.float32) / half)
    angles = 1000.0 * tvals[:, None] * freqs
    both = jnp.concatenate([jnp.cos(angles), jnp.sin(angles)], axis=1)
    return jax.nn.silu(both).astype(jnp.bfloat16)


def pack_kernel(idx_ref, emb_ref, mod_ref, lat_ref, out_ref, gate_ref, mods_ref):
    tokens = lat_ref.shape[0]
    out_ref[0:tokens, :] = lat_ref[...].astype(jnp.bfloat16)
    emb = emb_ref[...]
    for i in range(3):
        mods = jnp.dot(emb, mod_ref[i], preferred_element_type=jnp.float32)
        mods = mods.astype(jnp.bfloat16).astype(jnp.float32)
        if i < 2:
            mods_ref[i] = mods
        else:
            gate_ref[...] = mods
    slot = idx_ref[5]
    tail = out_ref.shape[0] - tokens
    which = lax.broadcasted_iota(jnp.int32, (tail, lat_ref.shape[1]), 0)
    block = jnp.where(which == 0, mods_ref[0, pl.ds(slot, 1), :], 0.0)
    block = jnp.where(which == 1, mods_ref[1, pl.ds(slot, 1), :], block)
    out_ref[tokens:, :] = block.astype(jnp.bfloat16)


def sort_kernel(qkv_hbm, out_hbm, to_ref, qkv_ref, out_ref, sems):
    loads = [
        pltpu.make_async_copy(qkv_hbm, qkv_ref, sems.at[0]),
        pltpu.make_async_copy(out_hbm, out_ref, sems.at[1]),
    ]
    for load in loads:
        load.start()
    for load in loads:
        load.wait()
    out_rows = out_ref[...].astype(jnp.float32)
    quarter = out_rows.shape[0] // NX
    for dest in range(NX):
        at = slice(dest % 2 * HD, (dest % 2 + 1) * HD)
        rows = [qkv_ref[i, :, at].astype(jnp.float32) for i in range(3)]
        rows = jnp.concatenate(rows, axis=1)
        some = out_rows[dest * quarter : (dest + 1) * quarter]
        to_ref[dest] = jnp.concatenate([rows, some], axis=0).astype(jnp.bfloat16)


def order_kernel(all_ref, to_ref):
    for x in range(NX):
        for z in range(NZ):
            row = (x * NZ + z) * 32
            rows = [all_ref[part, z, x].astype(jnp.float32) for part in range(NX)]
            to_ref[row : row + 32, :] = jnp.concatenate(rows, axis=0).astype(jnp.bfloat16)


def norm_kernel(idx_ref, *refs):
    xs, h_ref = refs[:8], refs[8]
    y, c = idx_ref[2], idx_ref[3]
    tokens, width = h_ref.shape[1], xs[0].shape[2]
    features = 8 * width
    for slot in range(2):
        total = jnp.zeros((tokens, 1), jnp.float32)
        for part in xs:
            total += jnp.sum(part[slot, 0:tokens, :].astype(jnp.float32), axis=-1, keepdims=True)
        mean = total / features
        total = jnp.zeros((tokens, 1), jnp.float32)
        for part in xs:
            cent = part[slot, 0:tokens, :].astype(jnp.float32) - mean
            total += jnp.sum(cent * cent, axis=-1, keepdims=True)
        inv = lax.rsqrt(total / features + 1e-06)
        for j in range(NY):
            for i in range(NC):
                part = xs[NC * j + i]
                place = lax.rem(y + NY - j, NY) * NC + lax.rem(c + i, NC)
                mods = part[slot, tokens : tokens + 16, :].astype(jnp.float32)
                cent = part[slot, 0:tokens, :].astype(jnp.float32) - mean
                hidden = cent * inv * (1.0 + mods[1:2]) + mods[0:1]
                at = pl.ds(pl.multiple_of(place * width, 128), width)
                h_ref[slot, :, at] = hidden.astype(jnp.bfloat16)


def attention_kernel(idx_ref, qg_ref, kg_ref, h_ref, all_ref, o_ref, rest_ref, w_ref):
    odd = lax.rem(idx_ref[0], 2)
    for x in range(NX):
        for z in range(NZ):
            row = (x * NZ + z) * 48
            rows = all_ref[z, x]
            w_ref[row : row + 48, :] = rows[0:48]
            rest_ref[z, x] = rows[48:56]
    for slot in range(2):
        qkv = jnp.dot(h_ref[slot], w_ref[...], preferred_element_type=jnp.float32)
        q = qkv[:, 0:HD]
        k = qkv[:, HD : 2 * HD]
        v = qkv[:, 2 * HD : 3 * HD].astype(jnp.bfloat16)
        qn = q * lax.rsqrt(jnp.mean(q * q, axis=-1, keepdims=True) + 1e-06) * qg_ref[...]
        kn = k * lax.rsqrt(jnp.mean(k * k, axis=-1, keepdims=True) + 1e-06) * kg_ref[...]
        scores = lax.dot_general(
            qn.astype(jnp.bfloat16),
            kn.astype(jnp.bfloat16),
            (((1,), (1,)), ((), ())),
            preferred_element_type=jnp.float32,
        ) * HD ** (-0.5)
        weights = jnp.exp(scores - jnp.max(scores, axis=-1, keepdims=True))
        probs = (weights / jnp.sum(weights, axis=-1, keepdims=True)).astype(jnp.bfloat16)
        out = jnp.dot(probs, v, preferred_element_type=jnp.float32)
        o_ref[lax.rem(odd + slot, 2)] = out.astype(jnp.bfloat16)


def project_kernel(idx_ref, win_ref, dt_ref, gate_ref, lat_ref, mine_ref, other_ref, w_ref, *refs):
    out_ref, a_ref, term_ref, run_ref = refs
    c = idx_ref[3]
    start, slide = win_ref[0], win_ref[1]
    for j in range(NY):
        for i, part in enumerate((mine_ref, other_ref)):
            for n in range(2):
                head = (j * NC + lax.rem(c + i, NC)) * 2 + n
                at = pl.ds(pl.multiple_of(head * HD, HD), HD)
                for m in range(2):
                    row = (2 * m + n) * 128
                    a_ref[m * 128 : (m + 1) * 128, at] = part[j, row : row + 128, :]
    proj = jnp.dot(a_ref[...], w_ref[...], preferred_element_type=jnp.float32)
    for slot in range(NX * NZ):
        row = slot // (2 * NZ) * 128 + slot % NZ * 8 + slot // NZ % 2 * 4
        gate = gate_ref[slot : slot + 1, :]
        term_ref[slot] = dt_ref[slot] * (gate * proj[row : row + 4, :])
    term_ref[start] = term_ref[start] + lat_ref[lax.rem(start, NZ)]
    count = NX * NZ

    def step(i, run):
        slot = lax.rem(start + i, count)
        run_ref[slot] = run
        return run + term_ref[slot]

    total = lax.fori_loop(
        0, count, step, jnp.zeros(run_ref.shape[1:], jnp.float32), unroll=8
    )

    def move(i, _):
        run_ref[lax.rem(start + i, count)] = total
        return 0

    lax.fori_loop(0, slide, move, 0)
    runs = run_ref[...]
    largest = jnp.max(jnp.max(jnp.abs(runs), axis=0), keepdims=True)
    power = jnp.clip(jnp.ceil(jnp.log2(largest)), -100.0, 100.0) - 14.0
    width = runs.shape[2]
    out_ref[:, :, 0:width] = runs * jnp.exp2(-power)[None]
    rest = out_ref.shape[2] - width
    out_ref[:, :, width:] = jnp.broadcast_to(power[None], runs.shape[:2] + (rest,))


def unscale_kernel(in_ref, out_ref):
    count, rows = in_ref.shape[0], in_ref.shape[1]
    width = out_ref.shape[1]
    scale = jnp.exp2(in_ref[:, :, width : width + 128])
    for g in range(width // 128):
        values = in_ref[:, :, g * 128 : (g + 1) * 128] * scale
        for i in range(count):
            out_ref[i * rows : (i + 1) * rows, g * 128 : (g + 1) * 128] = values[i]


def vmem():
    return pl.BlockSpec(memory_space=pltpu.VMEM)


def smem():
    return pl.BlockSpec(memory_space=pltpu.SMEM)


def params():
    return pltpu.CompilerParams(vmem_limit_bytes=VMEM_LIMIT)


def per_device(
    latents,
    timesteps,
    start_offset,
    slide_count,
    mod_weight,
    qkv_weight,
    out_weight,
    q_gain,
    k_gain,
):
    x, z, y, c = (lax.axis_index(a) for a in ("x", "z", "y", "c"))
    slot = x * NZ + z
    count = NX * NZ
    start, slide = start_offset[0], slide_count[0]
    grid = jnp.float32(48 * count)
    times = timesteps.astype(jnp.float32)
    tvals = times[:-1] / grid
    step_dts = (timesteps[:-1] - timesteps[1:]).astype(jnp.float32) / grid
    local = latents[0]
    tokens, width = local.shape

    sorted_rows = pl.pallas_call(
        sort_kernel,
        out_shape=jax.ShapeDtypeStruct((NX, 56, 3 * HD), jnp.bfloat16),
        in_specs=[pl.BlockSpec(memory_space=pl.ANY)] * 2,
        out_specs=vmem(),
        scratch_shapes=[
            pltpu.VMEM(qkv_weight.shape, jnp.bfloat16),
            pltpu.VMEM(out_weight.shape, jnp.bfloat16),
            pltpu.SemaphoreType.DMA((2,)),
        ],
        compiler_params=pltpu.CompilerParams(vmem_limit_bytes=61 * 1024 * 1024),
        name="sort",
    )(qkv_weight, out_weight)
    weights = lax.all_gather(lax.all_to_all(sorted_rows, "x", 0, 0, tiled=True), "z")

    idx = jnp.stack([x, z, y, c, start, slot]).astype(jnp.int32)
    emb = embed_time(tvals, mod_weight.shape[1])
    packed, gates = pl.pallas_call(
        pack_kernel,
        out_shape=(
            jax.ShapeDtypeStruct((tokens + 16, width), jnp.bfloat16),
            jax.ShapeDtypeStruct((count, width), jnp.float32),
        ),
        in_specs=[smem()] + [vmem()] * 3,
        out_specs=(vmem(), vmem()),
        scratch_shapes=[pltpu.VMEM((2, count, width), jnp.float32)],
        compiler_params=params(),
        name="pack",
    )(idx, emb, mod_weight, local)
    both = jnp.stack([packed, swap_pair(packed)])
    xs = [both] + [shift(both, "y", NY, j) for j in range(1, NY)]
    xs = [b for mine in xs for b in (mine, swap_core(mine))]
    hidden = pl.pallas_call(
        norm_kernel,
        out_shape=jax.ShapeDtypeStruct((2, tokens, 8 * width), jnp.bfloat16),
        in_specs=[smem()] + [vmem()] * 8,
        out_specs=vmem(),
        compiler_params=params(),
        name="norm",
    )(idx, *xs)

    rows = tokens // count
    first = local.astype(jnp.float16).reshape(NX, tokens // NX, width)
    first = lax.all_to_all(first, "x", 0, 0, tiled=True)
    first = lax.dynamic_index_in_dim(first, start // NZ, 0, keepdims=False)
    first = lax.all_to_all(first.reshape(NZ, rows, width), "z", 0, 0, tiled=True)
    weights, first, hidden = lax.optimization_barrier((weights, first, hidden))
    attn, out_rows = pl.pallas_call(
        attention_kernel,
        out_shape=(
            jax.ShapeDtypeStruct((2, tokens, HD), jnp.bfloat16),
            jax.ShapeDtypeStruct((NZ, NX, 8, width), jnp.bfloat16),
        ),
        in_specs=[smem()] + [vmem()] * 4,
        out_specs=(vmem(), vmem()),
        scratch_shapes=[pltpu.VMEM((48 * count, 3 * HD), jnp.bfloat16)],
        compiler_params=params(),
        name="attention",
    )(idx, q_gain[None], k_gain[None], hidden, weights)
    out_parts = lax.all_gather(out_rows, "x")
    attn = attn.reshape(2, count, rows, HD).transpose(1, 0, 2, 3).reshape(count, 2 * rows, HD)
    attn = lax.all_to_all(attn, STEP, 0, 0, tiled=True).reshape(count * 2 * rows, HD)
    mine = to_all(attn, "y", NY)
    out_rows = pl.pallas_call(
        order_kernel,
        out_shape=jax.ShapeDtypeStruct((2048, width), jnp.bfloat16),
        in_specs=[vmem()],
        out_specs=vmem(),
        compiler_params=params(),
        name="order",
    )(out_parts)
    sums = pl.pallas_call(
        project_kernel,
        out_shape=jax.ShapeDtypeStruct((count, rows, width + 128), jnp.float32),
        in_specs=[smem()] * 3 + [vmem()] * 5,
        out_specs=vmem(),
        scratch_shapes=[
            pltpu.VMEM((tokens, 2048), jnp.bfloat16),
            pltpu.VMEM((count, rows, width), jnp.float32),
            pltpu.VMEM((count, rows, width), jnp.float32),
        ],
        compiler_params=params(),
        name="project",
    )(idx, jnp.stack([start, slide]), step_dts, gates, first.astype(jnp.float32), mine, swap_core(mine), out_rows)
    back = lax.all_to_all(sums.astype(jnp.float16), STEP, 0, 0, tiled=True).astype(jnp.float32)
    return pl.pallas_call(
        unscale_kernel,
        out_shape=jax.ShapeDtypeStruct((tokens, width), jnp.float32),
        in_specs=[vmem()],
        out_specs=vmem(),
        compiler_params=params(),
        name="unscale",
    )(back)[None]


def solution(mesh):
    fine = Mesh(mesh.devices.reshape(NX, NZ, NY, NC), ("x", "z", "y", "c"))
    return jax.shard_map(
        per_device,
        mesh=fine,
        in_specs=(
            P(STEP, None, TP),
            P(),
            P(),
            P(),
            P(None, None, TP),
            P(None, STEP, TP),
            P(STEP, TP),
            P(),
            P(),
        ),
        out_specs=P(STEP, None, TP),
        check_vma=False,
    )
```

```python
import math

import jax
import jax.numpy as jnp
from jax import lax
from jax.experimental import pallas as pl
from jax.experimental.pallas import tpu as pltpu
from jax.sharding import Mesh
from jax.sharding import PartitionSpec as P

HD = 128
NX, NZ, NY, NC = 4, 16, 4, 2
STEP = ("x", "z")
TP = ("y", "c")
VMEM_LIMIT = 40 * 1024 * 1024


def shift(value, axis, size, by):
    return lax.ppermute(value, axis, [(i, (i + by) % size) for i in range(size)])


def swap_pair(value):
    return lax.ppermute(value, "x", [(i, i ^ 1) for i in range(NX)])


def swap_core(value):
    return lax.ppermute(value, "c", [(i, i ^ 1) for i in range(NC)])


def to_all(value, axis, size):
    return lax.all_to_all(jnp.broadcast_to(value[None], (size,) + value.shape), axis, 0, 0)


def embed_time(tvals, width):
    half = width // 2
    freqs = jnp.exp(-math.log(10000.0) * jnp.arange(half, dtype=jnp.float32) / half)
    angles = 1000.0 * tvals[:, None] * freqs
    both = jnp.concatenate([jnp.cos(angles), jnp.sin(angles)], axis=1)
    return jax.nn.silu(both).astype(jnp.bfloat16)


def pack_kernel(idx_ref, emb_ref, mod_ref, lat_ref, out_ref, gate_ref, mods_ref):
    tokens = lat_ref.shape[0]
    out_ref[0:tokens, :] = lat_ref[...].astype(jnp.bfloat16)
    emb = emb_ref[...]
    for i in range(3):
        mods = jnp.dot(emb, mod_ref[i], preferred_element_type=jnp.float32)
        mods = mods.astype(jnp.bfloat16).astype(jnp.float32)
        if i < 2:
            mods_ref[i] = mods
        else:
            gate_ref[...] = mods
    slot = idx_ref[5]
    tail = out_ref.shape[0] - tokens
    which = lax.broadcasted_iota(jnp.int32, (tail, lat_ref.shape[1]), 0)
    block = jnp.where(which == 0, mods_ref[0, pl.ds(slot, 1), :], 0.0)
    block = jnp.where(which == 1, mods_ref[1, pl.ds(slot, 1), :], block)
    out_ref[tokens:, :] = block.astype(jnp.bfloat16)


def sort_kernel(qkv_hbm, out_hbm, to_ref, qkv_ref, out_ref, sems):
    loads = [
        pltpu.make_async_copy(qkv_hbm, qkv_ref, sems.at[0]),
        pltpu.make_async_copy(out_hbm, out_ref, sems.at[1]),
    ]
    for load in loads:
        load.start()
    for load in loads:
        load.wait()
    out_rows = out_ref[...].astype(jnp.float32)
    quarter = out_rows.shape[0] // NX
    for dest in range(NX):
        at = slice(dest % 2 * HD, (dest % 2 + 1) * HD)
        rows = [qkv_ref[i, :, at].astype(jnp.float32) for i in range(3)]
        rows = jnp.concatenate(rows, axis=1)
        some = out_rows[dest * quarter : (dest + 1) * quarter]
        to_ref[dest] = jnp.concatenate([rows, some], axis=0).astype(jnp.bfloat16)


def order_kernel(all_ref, to_ref):
    for x in range(NX):
        for z in range(NZ):
            row = (x * NZ + z) * 32
            rows = [all_ref[part, z, x].astype(jnp.float32) for part in range(NX)]
            to_ref[row : row + 32, :] = jnp.concatenate(rows, axis=0).astype(jnp.bfloat16)


def norm_kernel(idx_ref, *refs):
    xs, h_ref = refs[:8], refs[8]
    y, c = idx_ref[2], idx_ref[3]
    tokens, width = h_ref.shape[1], xs[0].shape[2]
    features = 8 * width
    for slot in range(2):
        total = jnp.zeros((tokens, 1), jnp.float32)
        for part in xs:
            total += jnp.sum(part[slot, 0:tokens, :].astype(jnp.float32), axis=-1, keepdims=True)
        mean = total / features
        total = jnp.zeros((tokens, 1), jnp.float32)
        for part in xs:
            cent = part[slot, 0:tokens, :].astype(jnp.float32) - mean
            total += jnp.sum(cent * cent, axis=-1, keepdims=True)
        inv = lax.rsqrt(total / features + 1e-06)
        for j in range(NY):
            for i in range(NC):
                part = xs[NC * j + i]
                place = lax.rem(y + NY - j, NY) * NC + lax.rem(c + i, NC)
                mods = part[slot, tokens : tokens + 16, :].astype(jnp.float32)
                cent = part[slot, 0:tokens, :].astype(jnp.float32) - mean
                hidden = cent * inv * (1.0 + mods[1:2]) + mods[0:1]
                at = pl.ds(pl.multiple_of(place * width, 128), width)
                h_ref[slot, :, at] = hidden.astype(jnp.bfloat16)


def attention_kernel(idx_ref, qg_ref, kg_ref, h_ref, all_ref, o_ref, rest_ref, w_ref):
    odd = lax.rem(idx_ref[0], 2)
    for x in range(NX):
        for z in range(NZ):
            row = (x * NZ + z) * 48
            rows = all_ref[z, x]
            w_ref[row : row + 48, :] = rows[0:48]
            rest_ref[z, x] = rows[48:56]
    for slot in range(2):
        qkv = jnp.dot(h_ref[slot], w_ref[...], preferred_element_type=jnp.float32)
        q = qkv[:, 0:HD]
        k = qkv[:, HD : 2 * HD]
        v = qkv[:, 2 * HD : 3 * HD].astype(jnp.bfloat16)
        qn = q * lax.rsqrt(jnp.mean(q * q, axis=-1, keepdims=True) + 1e-06) * qg_ref[...]
        kn = k * lax.rsqrt(jnp.mean(k * k, axis=-1, keepdims=True) + 1e-06) * kg_ref[...]
        scores = lax.dot_general(
            qn.astype(jnp.bfloat16),
            kn.astype(jnp.bfloat16),
            (((1,), (1,)), ((), ())),
            preferred_element_type=jnp.float32,
        ) * HD ** (-0.5)
        weights = jnp.exp(scores - jnp.max(scores, axis=-1, keepdims=True))
        probs = (weights / jnp.sum(weights, axis=-1, keepdims=True)).astype(jnp.bfloat16)
        out = jnp.dot(probs, v, preferred_element_type=jnp.float32)
        o_ref[lax.rem(odd + slot, 2)] = out.astype(jnp.bfloat16)


def project_kernel(idx_ref, win_ref, dt_ref, gate_ref, lat_ref, mine_ref, other_ref, w_ref, *refs):
    out_ref, a_ref, term_ref, run_ref = refs
    c = idx_ref[3]
    start, slide = win_ref[0], win_ref[1]
    for j in range(NY):
        for i, part in enumerate((mine_ref, other_ref)):
            for n in range(2):
                head = (j * NC + lax.rem(c + i, NC)) * 2 + n
                at = pl.ds(pl.multiple_of(head * HD, HD), HD)
                for m in range(2):
                    row = (2 * m + n) * 128
                    a_ref[m * 128 : (m + 1) * 128, at] = part[j, row : row + 128, :]
    proj = jnp.dot(a_ref[...], w_ref[...], preferred_element_type=jnp.float32)
    for slot in range(NX * NZ):
        row = slot // (2 * NZ) * 128 + slot % NZ * 8 + slot // NZ % 2 * 4
        gate = gate_ref[slot : slot + 1, :]
        term_ref[slot] = dt_ref[slot] * (gate * proj[row : row + 4, :])
    term_ref[start] = term_ref[start] + lat_ref[lax.rem(start, NZ)]
    count = NX * NZ

    def step(i, run):
        slot = lax.rem(start + i, count)
        run_ref[slot] = run
        return run + term_ref[slot]

    total = lax.fori_loop(
        0, count, step, jnp.zeros(run_ref.shape[1:], jnp.float32), unroll=8
    )

    def move(i, _):
        run_ref[lax.rem(start + i, count)] = total
        return 0

    lax.fori_loop(0, slide, move, 0)
    runs = run_ref[...]
    largest = jnp.max(jnp.max(jnp.abs(runs), axis=0), keepdims=True)
    power = jnp.clip(jnp.ceil(jnp.log2(largest)), -100.0, 100.0) - 14.0
    width = runs.shape[2]
    out_ref[:, :, 0:width] = runs * jnp.exp2(-power)[None]
    rest = out_ref.shape[2] - width
    out_ref[:, :, width:] = jnp.broadcast_to(power[None], runs.shape[:2] + (rest,))


def unscale_kernel(in_ref, out_ref):
    count, rows = in_ref.shape[0], in_ref.shape[1]
    width = out_ref.shape[1]
    scale = jnp.exp2(in_ref[:, :, width : width + 128])
    for g in range(width // 128):
        values = in_ref[:, :, g * 128 : (g + 1) * 128] * scale
        for i in range(count):
            out_ref[i * rows : (i + 1) * rows, g * 128 : (g + 1) * 128] = values[i]


def vmem():
    return pl.BlockSpec(memory_space=pltpu.VMEM)


def smem():
    return pl.BlockSpec(memory_space=pltpu.SMEM)


def params():
    return pltpu.CompilerParams(vmem_limit_bytes=VMEM_LIMIT)


def per_device(
    latents,
    timesteps,
    start_offset,
    slide_count,
    mod_weight,
    qkv_weight,
    out_weight,
    q_gain,
    k_gain,
):
    x, z, y, c = (lax.axis_index(a) for a in ("x", "z", "y", "c"))
    slot = x * NZ + z
    count = NX * NZ
    start, slide = start_offset[0], slide_count[0]
    grid = jnp.float32(48 * count)
    times = timesteps.astype(jnp.float32)
    tvals = times[:-1] / grid
    step_dts = (timesteps[:-1] - timesteps[1:]).astype(jnp.float32) / grid
    local = latents[0]
    tokens, width = local.shape

    sorted_rows = pl.pallas_call(
        sort_kernel,
        out_shape=jax.ShapeDtypeStruct((NX, 56, 3 * HD), jnp.bfloat16),
        in_specs=[pl.BlockSpec(memory_space=pl.ANY)] * 2,
        out_specs=vmem(),
        scratch_shapes=[
            pltpu.VMEM(qkv_weight.shape, jnp.bfloat16),
            pltpu.VMEM(out_weight.shape, jnp.bfloat16),
            pltpu.SemaphoreType.DMA((2,)),
        ],
        compiler_params=pltpu.CompilerParams(vmem_limit_bytes=61 * 1024 * 1024),
        name="sort",
    )(qkv_weight, out_weight)
    weights = lax.all_gather(lax.all_to_all(sorted_rows, "x", 0, 0, tiled=True), "z")

    idx = jnp.stack([x, z, y, c, start, slot]).astype(jnp.int32)
    emb = embed_time(tvals, mod_weight.shape[1])
    packed, gates = pl.pallas_call(
        pack_kernel,
        out_shape=(
            jax.ShapeDtypeStruct((tokens + 16, width), jnp.bfloat16),
            jax.ShapeDtypeStruct((count, width), jnp.float32),
        ),
        in_specs=[smem()] + [vmem()] * 3,
        out_specs=(vmem(), vmem()),
        scratch_shapes=[pltpu.VMEM((2, count, width), jnp.float32)],
        compiler_params=params(),
        name="pack",
    )(idx, emb, mod_weight, local)
    both = jnp.stack([packed, swap_pair(packed)])
    xs = [both] + [shift(both, "y", NY, j) for j in range(1, NY)]
    xs = [b for mine in xs for b in (mine, swap_core(mine))]
    hidden = pl.pallas_call(
        norm_kernel,
        out_shape=jax.ShapeDtypeStruct((2, tokens, 8 * width), jnp.bfloat16),
        in_specs=[smem()] + [vmem()] * 8,
        out_specs=vmem(),
        compiler_params=params(),
        name="norm",
    )(idx, *xs)

    rows = tokens // count
    first = local.astype(jnp.float16).reshape(NX, tokens // NX, width)
    first = lax.all_to_all(first, "x", 0, 0, tiled=True)
    first = lax.dynamic_index_in_dim(first, start // NZ, 0, keepdims=False)
    first = lax.all_to_all(first.reshape(NZ, rows, width), "z", 0, 0, tiled=True)
    weights, first, hidden = lax.optimization_barrier((weights, first, hidden))
    attn, out_rows = pl.pallas_call(
        attention_kernel,
        out_shape=(
            jax.ShapeDtypeStruct((2, tokens, HD), jnp.bfloat16),
            jax.ShapeDtypeStruct((NZ, NX, 8, width), jnp.bfloat16),
        ),
        in_specs=[smem()] + [vmem()] * 4,
        out_specs=(vmem(), vmem()),
        scratch_shapes=[pltpu.VMEM((48 * count, 3 * HD), jnp.bfloat16)],
        compiler_params=params(),
        name="attention",
    )(idx, q_gain[None], k_gain[None], hidden, weights)
    out_parts = lax.all_gather(out_rows, "x")
    attn = attn.reshape(2, count, rows, HD).transpose(1, 0, 2, 3).reshape(count, 2 * rows, HD)
    attn = lax.all_to_all(attn, STEP, 0, 0, tiled=True).reshape(count * 2 * rows, HD)
    mine = to_all(attn, "y", NY)
    out_rows = pl.pallas_call(
        order_kernel,
        out_shape=jax.ShapeDtypeStruct((2048, width), jnp.bfloat16),
        in_specs=[vmem()],
        out_specs=vmem(),
        compiler_params=params(),
        name="order",
    )(out_parts)
    mine, out_rows = lax.optimization_barrier((mine, out_rows))
    sums = pl.pallas_call(
        project_kernel,
        out_shape=jax.ShapeDtypeStruct((count, rows, width + 128), jnp.float32),
        in_specs=[smem()] * 3 + [vmem()] * 5,
        out_specs=vmem(),
        scratch_shapes=[
            pltpu.VMEM((tokens, 2048), jnp.bfloat16),
            pltpu.VMEM((count, rows, width), jnp.float32),
            pltpu.VMEM((count, rows, width), jnp.float32),
        ],
        compiler_params=params(),
        name="project",
    )(idx, jnp.stack([start, slide]), step_dts, gates, first.astype(jnp.float32), mine, swap_core(mine), out_rows)
    back = lax.all_to_all(sums.astype(jnp.float16), STEP, 0, 0, tiled=True).astype(jnp.float32)
    return pl.pallas_call(
        unscale_kernel,
        out_shape=jax.ShapeDtypeStruct((tokens, width), jnp.float32),
        in_specs=[vmem()],
        out_specs=vmem(),
        compiler_params=params(),
        name="unscale",
    )(back)[None]


def solution(mesh):
    fine = Mesh(mesh.devices.reshape(NX, NZ, NY, NC), ("x", "z", "y", "c"))
    return jax.shard_map(
        per_device,
        mesh=fine,
        in_specs=(
            P(STEP, None, TP),
            P(),
            P(),
            P(),
            P(None, None, TP),
            P(None, STEP, TP),
            P(STEP, TP),
            P(),
            P(),
        ),
        out_specs=P(STEP, None, TP),
        check_vma=False,
    )
```

```python
import math

import jax
import jax.numpy as jnp
from jax import lax
from jax.experimental import pallas as pl
from jax.experimental.pallas import tpu as pltpu
from jax.sharding import Mesh
from jax.sharding import PartitionSpec as P

HD = 128
NX, NZ, NY, NC = 4, 16, 4, 2
STEP = ("x", "z")
TP = ("y", "c")
VMEM_LIMIT = 40 * 1024 * 1024


def shift(value, axis, size, by):
    return lax.ppermute(value, axis, [(i, (i + by) % size) for i in range(size)])


def swap_pair(value):
    return lax.ppermute(value, "x", [(i, i ^ 1) for i in range(NX)])


def swap_core(value):
    return lax.ppermute(value, "c", [(i, i ^ 1) for i in range(NC)])


def to_all(value, axis, size):
    return lax.all_to_all(jnp.broadcast_to(value[None], (size,) + value.shape), axis, 0, 0)


def embed_time(tvals, width):
    half = width // 2
    freqs = jnp.exp(-math.log(10000.0) * jnp.arange(half, dtype=jnp.float32) / half)
    angles = 1000.0 * tvals[:, None] * freqs
    both = jnp.concatenate([jnp.cos(angles), jnp.sin(angles)], axis=1)
    return jax.nn.silu(both).astype(jnp.bfloat16)


def pack_kernel(idx_ref, emb_ref, mod_ref, lat_ref, out_ref, gate_ref, mods_ref):
    tokens = lat_ref.shape[0]
    out_ref[0:tokens, :] = lat_ref[...].astype(jnp.bfloat16)
    emb = emb_ref[...]
    for i in range(3):
        mods = jnp.dot(emb, mod_ref[i], preferred_element_type=jnp.float32)
        mods = mods.astype(jnp.bfloat16).astype(jnp.float32)
        if i < 2:
            mods_ref[i] = mods
        else:
            gate_ref[...] = mods
    slot = idx_ref[5]
    tail = out_ref.shape[0] - tokens
    which = lax.broadcasted_iota(jnp.int32, (tail, lat_ref.shape[1]), 0)
    block = jnp.where(which == 0, mods_ref[0, pl.ds(slot, 1), :], 0.0)
    block = jnp.where(which == 1, mods_ref[1, pl.ds(slot, 1), :], block)
    out_ref[tokens:, :] = block.astype(jnp.bfloat16)


def sort_kernel(qkv_hbm, out_hbm, to_ref, qkv_ref, out_ref, sems):
    loads = [
        pltpu.make_async_copy(qkv_hbm, qkv_ref, sems.at[0]),
        pltpu.make_async_copy(out_hbm, out_ref, sems.at[1]),
    ]
    for load in loads:
        load.start()
    for load in loads:
        load.wait()
    out_rows = out_ref[...].astype(jnp.float32)
    quarter = out_rows.shape[0] // NX
    for dest in range(NX):
        at = slice(dest % 2 * HD, (dest % 2 + 1) * HD)
        rows = [qkv_ref[i, :, at].astype(jnp.float32) for i in range(3)]
        rows = jnp.concatenate(rows, axis=1)
        some = out_rows[dest * quarter : (dest + 1) * quarter]
        to_ref[dest] = jnp.concatenate([rows, some], axis=0).astype(jnp.bfloat16)


def order_kernel(all_ref, to_ref):
    for x in range(NX):
        for z in range(NZ):
            row = (x * NZ + z) * 32
            rows = [all_ref[part, z, x].astype(jnp.float32) for part in range(NX)]
            to_ref[row : row + 32, :] = jnp.concatenate(rows, axis=0).astype(jnp.bfloat16)


def norm_kernel(idx_ref, *refs):
    xs, h_ref = refs[:8], refs[8]
    y, c = idx_ref[2], idx_ref[3]
    tokens, width = h_ref.shape[1], xs[0].shape[2]
    features = 8 * width
    for slot in range(2):
        total = jnp.zeros((tokens, 1), jnp.float32)
        for part in xs:
            total += jnp.sum(part[slot, 0:tokens, :].astype(jnp.float32), axis=-1, keepdims=True)
        mean = total / features
        total = jnp.zeros((tokens, 1), jnp.float32)
        for part in xs:
            cent = part[slot, 0:tokens, :].astype(jnp.float32) - mean
            total += jnp.sum(cent * cent, axis=-1, keepdims=True)
        inv = lax.rsqrt(total / features + 1e-06)
        for j in range(NY):
            for i in range(NC):
                part = xs[NC * j + i]
                place = lax.rem(y + NY - j, NY) * NC + lax.rem(c + i, NC)
                mods = part[slot, tokens : tokens + 16, :].astype(jnp.float32)
                cent = part[slot, 0:tokens, :].astype(jnp.float32) - mean
                hidden = cent * inv * (1.0 + mods[1:2]) + mods[0:1]
                at = pl.ds(pl.multiple_of(place * width, 128), width)
                h_ref[slot, :, at] = hidden.astype(jnp.bfloat16)


def attention_kernel(idx_ref, qg_ref, kg_ref, h_ref, all_ref, o_ref, rest_ref, w_ref):
    odd = lax.rem(idx_ref[0], 2)
    for x in range(NX):
        for z in range(NZ):
            row = (x * NZ + z) * 48
            rows = all_ref[z, x]
            w_ref[row : row + 48, :] = rows[0:48]
            rest_ref[z, x] = rows[48:56]
    for slot in range(2):
        qkv = jnp.dot(h_ref[slot], w_ref[...], preferred_element_type=jnp.float32)
        q = qkv[:, 0:HD]
        k = qkv[:, HD : 2 * HD]
        v = qkv[:, 2 * HD : 3 * HD].astype(jnp.bfloat16)
        qn = q * lax.rsqrt(jnp.mean(q * q, axis=-1, keepdims=True) + 1e-06) * qg_ref[...]
        kn = k * lax.rsqrt(jnp.mean(k * k, axis=-1, keepdims=True) + 1e-06) * kg_ref[...]
        scores = lax.dot_general(
            qn.astype(jnp.bfloat16),
            kn.astype(jnp.bfloat16),
            (((1,), (1,)), ((), ())),
            preferred_element_type=jnp.float32,
        ) * HD ** (-0.5)
        weights = jnp.exp(scores - jnp.max(scores, axis=-1, keepdims=True))
        probs = (weights / jnp.sum(weights, axis=-1, keepdims=True)).astype(jnp.bfloat16)
        out = jnp.dot(probs, v, preferred_element_type=jnp.float32)
        o_ref[lax.rem(odd + slot, 2)] = out.astype(jnp.bfloat16)


def project_kernel(idx_ref, win_ref, dt_ref, gate_ref, lat_ref, mine_ref, other_ref, w_ref, *refs):
    out_ref, a_ref, term_ref, run_ref = refs
    c = idx_ref[3]
    start, slide = win_ref[0], win_ref[1]
    for j in range(NY):
        for i, part in enumerate((mine_ref, other_ref)):
            for n in range(2):
                head = (j * NC + lax.rem(c + i, NC)) * 2 + n
                at = pl.ds(pl.multiple_of(head * HD, HD), HD)
                for m in range(2):
                    row = (2 * m + n) * 128
                    a_ref[m * 128 : (m + 1) * 128, at] = part[j, row : row + 128, :]
    proj = jnp.dot(a_ref[...], w_ref[...], preferred_element_type=jnp.float32)
    for slot in range(NX * NZ):
        row = slot // (2 * NZ) * 128 + slot % NZ * 8 + slot // NZ % 2 * 4
        gate = gate_ref[slot : slot + 1, :]
        term_ref[slot] = dt_ref[slot] * (gate * proj[row : row + 4, :])
    term_ref[start] = term_ref[start] + lat_ref[lax.rem(start, NZ)]
    count = NX * NZ

    def step(i, run):
        slot = lax.rem(start + i, count)
        run_ref[slot] = run
        return run + term_ref[slot]

    total = lax.fori_loop(
        0, count, step, jnp.zeros(run_ref.shape[1:], jnp.float32), unroll=8
    )

    def move(i, _):
        run_ref[lax.rem(start + i, count)] = total
        return 0

    lax.fori_loop(0, slide, move, 0)
    runs = run_ref[...]
    largest = jnp.max(jnp.max(jnp.abs(runs), axis=0), keepdims=True)
    power = jnp.clip(jnp.ceil(jnp.log2(largest)), -100.0, 100.0) - 14.0
    width = runs.shape[2]
    runs = runs * jnp.exp2(-power)[None]
    half = runs.shape[1] // 2
    for token in range(runs.shape[1]):
        row, at = token // half, token % half * width
        out_ref[:, row : row + 1, at : at + width] = runs[:, token : token + 1, :]
    at = half * width
    out_ref[:, :, at:] = jnp.broadcast_to(power[None], (out_ref.shape[0], 2, 128))


def unscale_kernel(in_ref, out_ref):
    count, width = in_ref.shape[0], out_ref.shape[1]
    rows = out_ref.shape[0] // count
    half = rows // 2
    scale = jnp.exp2(in_ref[:, :, half * width :])
    for token in range(rows):
        row, at = token // half, token % half * width
        for g in range(width // 128):
            part = in_ref[:, row : row + 1, at + g * 128 : at + (g + 1) * 128]
            values = part * scale[:, row : row + 1, :]
            for i in range(count):
                to = i * rows + token
                out_ref[to : to + 1, g * 128 : (g + 1) * 128] = values[i]


def vmem():
    return pl.BlockSpec(memory_space=pltpu.VMEM)


def smem():
    return pl.BlockSpec(memory_space=pltpu.SMEM)


def params():
    return pltpu.CompilerParams(vmem_limit_bytes=VMEM_LIMIT)


def per_device(
    latents,
    timesteps,
    start_offset,
    slide_count,
    mod_weight,
    qkv_weight,
    out_weight,
    q_gain,
    k_gain,
):
    x, z, y, c = (lax.axis_index(a) for a in ("x", "z", "y", "c"))
    slot = x * NZ + z
    count = NX * NZ
    start, slide = start_offset[0], slide_count[0]
    grid = jnp.float32(48 * count)
    times = timesteps.astype(jnp.float32)
    tvals = times[:-1] / grid
    step_dts = (timesteps[:-1] - timesteps[1:]).astype(jnp.float32) / grid
    local = latents[0]
    tokens, width = local.shape

    sorted_rows = pl.pallas_call(
        sort_kernel,
        out_shape=jax.ShapeDtypeStruct((NX, 56, 3 * HD), jnp.bfloat16),
        in_specs=[pl.BlockSpec(memory_space=pl.ANY)] * 2,
        out_specs=vmem(),
        scratch_shapes=[
            pltpu.VMEM(qkv_weight.shape, jnp.bfloat16),
            pltpu.VMEM(out_weight.shape, jnp.bfloat16),
            pltpu.SemaphoreType.DMA((2,)),
        ],
        compiler_params=pltpu.CompilerParams(vmem_limit_bytes=61 * 1024 * 1024),
        name="sort",
    )(qkv_weight, out_weight)
    weights = lax.all_gather(lax.all_to_all(sorted_rows, "x", 0, 0, tiled=True), "z")

    idx = jnp.stack([x, z, y, c, start, slot]).astype(jnp.int32)
    emb = embed_time(tvals, mod_weight.shape[1])
    packed, gates = pl.pallas_call(
        pack_kernel,
        out_shape=(
            jax.ShapeDtypeStruct((tokens + 16, width), jnp.bfloat16),
            jax.ShapeDtypeStruct((count, width), jnp.float32),
        ),
        in_specs=[smem()] + [vmem()] * 3,
        out_specs=(vmem(), vmem()),
        scratch_shapes=[pltpu.VMEM((2, count, width), jnp.float32)],
        compiler_params=params(),
        name="pack",
    )(idx, emb, mod_weight, local)
    both = jnp.stack([packed, swap_pair(packed)])
    xs = [both] + [shift(both, "y", NY, j) for j in range(1, NY)]
    xs = [b for mine in xs for b in (mine, swap_core(mine))]
    hidden = pl.pallas_call(
        norm_kernel,
        out_shape=jax.ShapeDtypeStruct((2, tokens, 8 * width), jnp.bfloat16),
        in_specs=[smem()] + [vmem()] * 8,
        out_specs=vmem(),
        compiler_params=params(),
        name="norm",
    )(idx, *xs)

    rows = tokens // count
    first = local.astype(jnp.float16).reshape(NX, tokens // NX, width)
    first = lax.all_to_all(first, "x", 0, 0, tiled=True)
    first = lax.dynamic_index_in_dim(first, start // NZ, 0, keepdims=False)
    first = lax.all_to_all(first.reshape(NZ, rows, width), "z", 0, 0, tiled=True)
    weights, first, hidden = lax.optimization_barrier((weights, first, hidden))
    attn, out_rows = pl.pallas_call(
        attention_kernel,
        out_shape=(
            jax.ShapeDtypeStruct((2, tokens, HD), jnp.bfloat16),
            jax.ShapeDtypeStruct((NZ, NX, 8, width), jnp.bfloat16),
        ),
        in_specs=[smem()] + [vmem()] * 4,
        out_specs=(vmem(), vmem()),
        scratch_shapes=[pltpu.VMEM((48 * count, 3 * HD), jnp.bfloat16)],
        compiler_params=params(),
        name="attention",
    )(idx, q_gain[None], k_gain[None], hidden, weights)
    out_parts = lax.all_gather(out_rows, "x")
    attn = attn.reshape(2, count, rows, HD).transpose(1, 0, 2, 3).reshape(count, 2 * rows, HD)
    attn = lax.all_to_all(attn, STEP, 0, 0, tiled=True).reshape(count * 2 * rows, HD)
    mine = to_all(attn, "y", NY)
    out_rows = pl.pallas_call(
        order_kernel,
        out_shape=jax.ShapeDtypeStruct((2048, width), jnp.bfloat16),
        in_specs=[vmem()],
        out_specs=vmem(),
        compiler_params=params(),
        name="order",
    )(out_parts)
    sums = pl.pallas_call(
        project_kernel,
        out_shape=jax.ShapeDtypeStruct((count, 2, rows // 2 * width + 128), jnp.float32),
        in_specs=[smem()] * 3 + [vmem()] * 5,
        out_specs=vmem(),
        scratch_shapes=[
            pltpu.VMEM((tokens, 2048), jnp.bfloat16),
            pltpu.VMEM((count, rows, width), jnp.float32),
            pltpu.VMEM((count, rows, width), jnp.float32),
        ],
        compiler_params=params(),
        name="project",
    )(idx, jnp.stack([start, slide]), step_dts, gates, first.astype(jnp.float32), mine, swap_core(mine), out_rows)
    back = lax.all_to_all(sums.astype(jnp.float16), STEP, 0, 0, tiled=True).astype(jnp.float32)
    return pl.pallas_call(
        unscale_kernel,
        out_shape=jax.ShapeDtypeStruct((tokens, width), jnp.float32),
        in_specs=[vmem()],
        out_specs=vmem(),
        compiler_params=params(),
        name="unscale",
    )(back)[None]


def solution(mesh):
    fine = Mesh(mesh.devices.reshape(NX, NZ, NY, NC), ("x", "z", "y", "c"))
    return jax.shard_map(
        per_device,
        mesh=fine,
        in_specs=(
            P(STEP, None, TP),
            P(),
            P(),
            P(),
            P(None, None, TP),
            P(None, STEP, TP),
            P(STEP, TP),
            P(),
            P(),
        ),
        out_specs=P(STEP, None, TP),
        check_vma=False,
    )
```

```python
import math

import jax
import jax.numpy as jnp
from jax import lax
from jax.experimental import pallas as pl
from jax.experimental.pallas import tpu as pltpu
from jax.sharding import Mesh
from jax.sharding import PartitionSpec as P

HD = 128
NX, NZ, NY, NC = 4, 16, 4, 2
STEP = ("x", "z")
TP = ("y", "c")
VMEM_LIMIT = 40 * 1024 * 1024


def shift(value, axis, size, by):
    return lax.ppermute(value, axis, [(i, (i + by) % size) for i in range(size)])


def swap_pair(value):
    return lax.ppermute(value, "x", [(i, i ^ 1) for i in range(NX)])


def swap_core(value):
    return lax.ppermute(value, "c", [(i, i ^ 1) for i in range(NC)])


def to_all(value, axis, size):
    return lax.all_to_all(jnp.broadcast_to(value[None], (size,) + value.shape), axis, 0, 0)


def embed_time(tvals, width):
    half = width // 2
    freqs = jnp.exp(-math.log(10000.0) * jnp.arange(half, dtype=jnp.float32) / half)
    angles = 1000.0 * tvals[:, None] * freqs
    both = jnp.concatenate([jnp.cos(angles), jnp.sin(angles)], axis=1)
    return jax.nn.silu(both).astype(jnp.bfloat16)


def pack_kernel(idx_ref, emb_ref, mod_ref, lat_ref, out_ref, gate_ref, mods_ref):
    tokens = lat_ref.shape[0]
    out_ref[0:tokens, :] = lat_ref[...].astype(jnp.bfloat16)
    emb = emb_ref[...]
    for i in range(3):
        mods = jnp.dot(emb, mod_ref[i], preferred_element_type=jnp.float32)
        mods = mods.astype(jnp.bfloat16).astype(jnp.float32)
        if i < 2:
            mods_ref[i] = mods
        else:
            gate_ref[...] = mods
    slot = idx_ref[5]
    tail = out_ref.shape[0] - tokens
    which = lax.broadcasted_iota(jnp.int32, (tail, lat_ref.shape[1]), 0)
    block = jnp.where(which == 0, mods_ref[0, pl.ds(slot, 1), :], 0.0)
    block = jnp.where(which == 1, mods_ref[1, pl.ds(slot, 1), :], block)
    out_ref[tokens:, :] = block.astype(jnp.bfloat16)


def sort_kernel(qkv_hbm, out_hbm, to_ref, qkv_ref, out_ref, sems):
    loads = [
        pltpu.make_async_copy(qkv_hbm, qkv_ref, sems.at[0]),
        pltpu.make_async_copy(out_hbm, out_ref, sems.at[1]),
    ]
    for load in loads:
        load.start()
    for load in loads:
        load.wait()
    out_rows = out_ref[...].astype(jnp.float32)
    quarter = out_rows.shape[0] // NX
    for dest in range(NX):
        at = slice(dest % 2 * HD, (dest % 2 + 1) * HD)
        rows = [qkv_ref[i, :, at].astype(jnp.float32) for i in range(3)]
        rows = jnp.concatenate(rows, axis=1)
        some = out_rows[dest * quarter : (dest + 1) * quarter]
        to_ref[dest] = jnp.concatenate([rows, some], axis=0).astype(jnp.bfloat16)


def order_kernel(all_ref, to_ref):
    for x in range(NX):
        for z in range(NZ):
            row = (x * NZ + z) * 32
            rows = [all_ref[part, z, x].astype(jnp.float32) for part in range(NX)]
            to_ref[row : row + 32, :] = jnp.concatenate(rows, axis=0).astype(jnp.bfloat16)


def norm_kernel(idx_ref, *refs):
    xs, h_ref = refs[:8], refs[8]
    y, c = idx_ref[2], idx_ref[3]
    tokens, width = h_ref.shape[1], xs[0].shape[2]
    features = 8 * width
    for slot in range(2):
        total = jnp.zeros((tokens, 1), jnp.float32)
        for part in xs:
            total += jnp.sum(part[slot, 0:tokens, :].astype(jnp.float32), axis=-1, keepdims=True)
        mean = total / features
        total = jnp.zeros((tokens, 1), jnp.float32)
        for part in xs:
            cent = part[slot, 0:tokens, :].astype(jnp.float32) - mean
            total += jnp.sum(cent * cent, axis=-1, keepdims=True)
        inv = lax.rsqrt(total / features + 1e-06)
        for j in range(NY):
            for i in range(NC):
                part = xs[NC * j + i]
                place = lax.rem(y + NY - j, NY) * NC + lax.rem(c + i, NC)
                mods = part[slot, tokens : tokens + 16, :].astype(jnp.float32)
                cent = part[slot, 0:tokens, :].astype(jnp.float32) - mean
                hidden = cent * inv * (1.0 + mods[1:2]) + mods[0:1]
                at = pl.ds(pl.multiple_of(place * width, 128), width)
                h_ref[slot, :, at] = hidden.astype(jnp.bfloat16)


def attention_kernel(idx_ref, qg_ref, kg_ref, h_ref, all_ref, o_ref, rest_ref, w_ref):
    odd = lax.rem(idx_ref[0], 2)
    for x in range(NX):
        for z in range(NZ):
            row = (x * NZ + z) * 48
            rows = all_ref[z, x]
            w_ref[row : row + 48, :] = rows[0:48]
            rest_ref[z, x] = rows[48:56]
    for slot in range(2):
        qkv = jnp.dot(h_ref[slot], w_ref[...], preferred_element_type=jnp.float32)
        q = qkv[:, 0:HD]
        k = qkv[:, HD : 2 * HD]
        v = qkv[:, 2 * HD : 3 * HD].astype(jnp.bfloat16)
        qn = q * lax.rsqrt(jnp.mean(q * q, axis=-1, keepdims=True) + 1e-06) * qg_ref[...]
        kn = k * lax.rsqrt(jnp.mean(k * k, axis=-1, keepdims=True) + 1e-06) * kg_ref[...]
        scores = lax.dot_general(
            qn.astype(jnp.bfloat16),
            kn.astype(jnp.bfloat16),
            (((1,), (1,)), ((), ())),
            preferred_element_type=jnp.float32,
        ) * HD ** (-0.5)
        weights = jnp.exp(scores - jnp.max(scores, axis=-1, keepdims=True))
        probs = (weights / jnp.sum(weights, axis=-1, keepdims=True)).astype(jnp.bfloat16)
        out = jnp.dot(probs, v, preferred_element_type=jnp.float32)
        o_ref[lax.rem(odd + slot, 2)] = out.astype(jnp.bfloat16)


def project_kernel(idx_ref, win_ref, dt_ref, gate_ref, lat_ref, mine_ref, other_ref, w_ref, *refs):
    out_ref, a_ref, term_ref, run_ref = refs
    c = idx_ref[3]
    start, slide = win_ref[0], win_ref[1]
    for j in range(NY):
        for i, part in enumerate((mine_ref, other_ref)):
            for n in range(2):
                head = (j * NC + lax.rem(c + i, NC)) * 2 + n
                at = pl.ds(pl.multiple_of(head * HD, HD), HD)
                for m in range(2):
                    row = (2 * m + n) * 128
                    a_ref[m * 128 : (m + 1) * 128, at] = part[j, row : row + 128, :]
    proj = jnp.dot(a_ref[...], w_ref[...], preferred_element_type=jnp.float32)
    for slot in range(NX * NZ):
        row = slot // (2 * NZ) * 128 + slot % NZ * 8 + slot // NZ % 2 * 4
        gate = gate_ref[slot : slot + 1, :]
        term_ref[slot] = dt_ref[slot] * (gate * proj[row : row + 4, :])
    term_ref[start] = term_ref[start] + lat_ref[lax.rem(start, NZ)]
    count = NX * NZ

    def step(i, run):
        slot = lax.rem(start + i, count)
        run_ref[slot] = run
        return run + term_ref[slot]

    total = lax.fori_loop(
        0, count, step, jnp.zeros(run_ref.shape[1:], jnp.float32), unroll=32
    )

    def move(i, _):
        run_ref[lax.rem(start + i, count)] = total
        return 0

    lax.fori_loop(0, slide, move, 0)
    runs = run_ref[...]
    largest = jnp.max(jnp.max(jnp.abs(runs), axis=0), keepdims=True)
    power = jnp.clip(jnp.ceil(jnp.log2(largest)), -100.0, 100.0) - 14.0
    width = runs.shape[2]
    runs = runs * jnp.exp2(-power)[None]
    half = runs.shape[1] // 2
    for token in range(runs.shape[1]):
        row, at = token // half, token % half * width
        out_ref[:, row : row + 1, at : at + width] = runs[:, token : token + 1, :]
    at = half * width
    out_ref[:, :, at:] = jnp.broadcast_to(power[None], (out_ref.shape[0], 2, 128))


def unscale_kernel(in_ref, out_ref):
    count, width = in_ref.shape[0], out_ref.shape[1]
    rows = out_ref.shape[0] // count
    half = rows // 2
    scale = jnp.exp2(in_ref[:, :, half * width :])
    for g in range(width // 128):
        parts = []
        for token in range(rows):
            row, at = token // half, token % half * width + g * 128
            parts.append(in_ref[:, row : row + 1, at : at + 128] * scale[:, row : row + 1, :])
        values = jnp.concatenate(parts, axis=1)
        for i in range(count):
            out_ref[i * rows : (i + 1) * rows, g * 128 : (g + 1) * 128] = values[i]


def vmem():
    return pl.BlockSpec(memory_space=pltpu.VMEM)


def smem():
    return pl.BlockSpec(memory_space=pltpu.SMEM)


def params():
    return pltpu.CompilerParams(vmem_limit_bytes=VMEM_LIMIT)


def per_device(
    latents,
    timesteps,
    start_offset,
    slide_count,
    mod_weight,
    qkv_weight,
    out_weight,
    q_gain,
    k_gain,
):
    x, z, y, c = (lax.axis_index(a) for a in ("x", "z", "y", "c"))
    slot = x * NZ + z
    count = NX * NZ
    start, slide = start_offset[0], slide_count[0]
    grid = jnp.float32(48 * count)
    times = timesteps.astype(jnp.float32)
    tvals = times[:-1] / grid
    step_dts = (timesteps[:-1] - timesteps[1:]).astype(jnp.float32) / grid
    local = latents[0]
    tokens, width = local.shape

    sorted_rows = pl.pallas_call(
        sort_kernel,
        out_shape=jax.ShapeDtypeStruct((NX, 56, 3 * HD), jnp.bfloat16),
        in_specs=[pl.BlockSpec(memory_space=pl.ANY)] * 2,
        out_specs=vmem(),
        scratch_shapes=[
            pltpu.VMEM(qkv_weight.shape, jnp.bfloat16),
            pltpu.VMEM(out_weight.shape, jnp.bfloat16),
            pltpu.SemaphoreType.DMA((2,)),
        ],
        compiler_params=pltpu.CompilerParams(vmem_limit_bytes=61 * 1024 * 1024),
        name="sort",
    )(qkv_weight, out_weight)
    weights = lax.all_gather(lax.all_to_all(sorted_rows, "x", 0, 0, tiled=True), "z")

    idx = jnp.stack([x, z, y, c, start, slot]).astype(jnp.int32)
    emb = embed_time(tvals, mod_weight.shape[1])
    packed, gates = pl.pallas_call(
        pack_kernel,
        out_shape=(
            jax.ShapeDtypeStruct((tokens + 16, width), jnp.bfloat16),
            jax.ShapeDtypeStruct((count, width), jnp.float32),
        ),
        in_specs=[smem()] + [vmem()] * 3,
        out_specs=(vmem(), vmem()),
        scratch_shapes=[pltpu.VMEM((2, count, width), jnp.float32)],
        compiler_params=params(),
        name="pack",
    )(idx, emb, mod_weight, local)
    both = jnp.stack([packed, swap_pair(packed)])
    xs = [both] + [shift(both, "y", NY, j) for j in range(1, NY)]
    xs = [b for mine in xs for b in (mine, swap_core(mine))]
    hidden = pl.pallas_call(
        norm_kernel,
        out_shape=jax.ShapeDtypeStruct((2, tokens, 8 * width), jnp.bfloat16),
        in_specs=[smem()] + [vmem()] * 8,
        out_specs=vmem(),
        compiler_params=params(),
        name="norm",
    )(idx, *xs)

    rows = tokens // count
    first = local.astype(jnp.float16).reshape(NX, tokens // NX, width)
    first = lax.all_to_all(first, "x", 0, 0, tiled=True)
    first = lax.dynamic_index_in_dim(first, start // NZ, 0, keepdims=False)
    first = lax.all_to_all(first.reshape(NZ, rows, width), "z", 0, 0, tiled=True)
    weights, first, hidden = lax.optimization_barrier((weights, first, hidden))
    attn, out_rows = pl.pallas_call(
        attention_kernel,
        out_shape=(
            jax.ShapeDtypeStruct((2, tokens, HD), jnp.bfloat16),
            jax.ShapeDtypeStruct((NZ, NX, 8, width), jnp.bfloat16),
        ),
        in_specs=[smem()] + [vmem()] * 4,
        out_specs=(vmem(), vmem()),
        scratch_shapes=[pltpu.VMEM((48 * count, 3 * HD), jnp.bfloat16)],
        compiler_params=params(),
        name="attention",
    )(idx, q_gain[None], k_gain[None], hidden, weights)
    out_parts = lax.all_gather(out_rows, "x")
    attn = attn.reshape(2, count, rows, HD).transpose(1, 0, 2, 3).reshape(count, 2 * rows, HD)
    attn = lax.all_to_all(attn, STEP, 0, 0, tiled=True).reshape(count * 2 * rows, HD)
    mine = to_all(attn, "y", NY)
    out_rows = pl.pallas_call(
        order_kernel,
        out_shape=jax.ShapeDtypeStruct((2048, width), jnp.bfloat16),
        in_specs=[vmem()],
        out_specs=vmem(),
        compiler_params=params(),
        name="order",
    )(out_parts)
    sums = pl.pallas_call(
        project_kernel,
        out_shape=jax.ShapeDtypeStruct((count, 2, rows // 2 * width + 128), jnp.float32),
        in_specs=[smem()] * 3 + [vmem()] * 5,
        out_specs=vmem(),
        scratch_shapes=[
            pltpu.VMEM((tokens, 2048), jnp.bfloat16),
            pltpu.VMEM((count, rows, width), jnp.float32),
            pltpu.VMEM((count, rows, width), jnp.float32),
        ],
        compiler_params=params(),
        name="project",
    )(idx, jnp.stack([start, slide]), step_dts, gates, first.astype(jnp.float32), mine, swap_core(mine), out_rows)
    back = lax.all_to_all(sums.astype(jnp.float16), STEP, 0, 0, tiled=True).astype(jnp.float32)
    return pl.pallas_call(
        unscale_kernel,
        out_shape=jax.ShapeDtypeStruct((tokens, width), jnp.float32),
        in_specs=[vmem()],
        out_specs=vmem(),
        compiler_params=params(),
        name="unscale",
    )(back)[None]


def solution(mesh):
    fine = Mesh(mesh.devices.reshape(NX, NZ, NY, NC), ("x", "z", "y", "c"))
    return jax.shard_map(
        per_device,
        mesh=fine,
        in_specs=(
            P(STEP, None, TP),
            P(),
            P(),
            P(),
            P(None, None, TP),
            P(None, STEP, TP),
            P(STEP, TP),
            P(),
            P(),
        ),
        out_specs=P(STEP, None, TP),
        check_vma=False,
    )
```
